128 devices in a mesh: dp: 4 (over x), leaf: 32 (over z, y, core).
Axes of the slice: x: 4, y: 4, z: 4, core: 2. Of those that a mesh axis runs over, the one named last changes fastest.
Arguments:
- queries: bfloat16 [32768, 3584], P(('dp', 'leaf')), may hold values from -72 to 72
- branch_keys: bfloat16 [32768, 512], P(('dp', 'leaf')), may hold values from -6 to 6
- branch_value_rows: bfloat16 [32768, 512], P(('dp', 'leaf')), may hold values from -6 to 6
- attention_output: bfloat16 [32768, 3584], P(('dp', 'leaf')), may hold values from -1.75 to 1.75
- output_gradient: bfloat16 [32768, 3584], P(('dp', 'leaf')), may hold values from -96 to 96
- anc_states: bfloat16 [16384, 3584], P(('dp', 'leaf')), may hold values from -24 to 24
- key_matrix: bfloat16 [3584, 512], replicated, may hold values from -0.09375 to 0.09375
- value_matrix: bfloat16 [3584, 512], replicated, may hold values from -0.09375 to 0.09375
- anc_blocks: int32 [128, 16], P(('dp', 'leaf')), may hold values from 0 to 63, as said below
- anc_count: int32 [128], P(('dp', 'leaf')), may hold values from 12 to 16, as said below
Outputs:
- query_grad: bfloat16 [32768, 3584], P(('dp', 'leaf'))
- branch_key_grad: bfloat16 [32768, 512], P(('dp', 'leaf'))
- branch_value_grad: bfloat16 [32768, 512], P(('dp', 'leaf'))
- anc_state_grad: bfloat16 [16384, 3584], P(('dp', 'leaf'))
- key_weight_grad: float32 [3584, 512], P(('dp', 'leaf'))
- value_weight_grad: float32 [3584, 512], P(('dp', 'leaf'))
The draws below stay inside these ranges and needn't reach their ends.
Inputs may be any that keep to these rules, and one draw needn't show every extreme that they name: `anc_blocks`: block b of a dp group is held by leaf index b // 2 of that group as its local block b % 2. The 16 entries of one device are distinct, and at most 1 of them are held by one leaf index. Slots 0 to anc_count - 1 of a device's list are live, the others are ignored. In every dp group some device has 16 live slots.
All inputs are finite; a program needn't handle non-finite values.
Results may differ from the reference program's by a relative error of at most 0.022.
Values may be sent and summed in bfloat16 or wider, within the bound.
A program may use at most 192 MiB of HBM per device.

```python
import math
import jax
import jax.numpy as jnp
from jax import lax

MODEL_WIDTH = 3584
QUERY_HEADS = 28
KEY_VALUE_HEADS = 4
HEAD_SIZE = 128
BRANCH_TOKENS = 256
NA = 16
BLK = 64
OWN = 2
N_DP = 4
N_LEAF = 32


def paired_draw(key):
    base = jax.random.fold_in(key, 11)
    row_total = N_DP * N_LEAF * BRANCH_TOKENS
    query_key, key_random_seed = jax.random.split(base, 2)
    queries = jnp.clip(jax.random.normal(query_key, (row_total, QUERY_HEADS * HEAD_SIZE), jnp.float32), -6.0, 6.0)
    key_tokens = jnp.clip(jax.random.normal(key_random_seed, (row_total, KEY_VALUE_HEADS * HEAD_SIZE), jnp.float32), -6.0, 6.0)
    return (queries, key_tokens)


def draw_queries(key, part):
    return paired_draw(key)[0].astype(jnp.bfloat16)


def draw_branch_keys(key, part):
    return paired_draw(key)[1].astype(jnp.bfloat16)


def one_order(order_key):
    return jax.random.permutation(order_key, N_LEAF)


def draw_anc_blocks(key, part):
    shards = N_DP * N_LEAF
    order_keys = jax.random.split(jax.random.fold_in(key, 21), shards)
    orders = jax.vmap(one_order)(order_keys).astype(jnp.int32)
    offsets = jax.random.randint(jax.random.fold_in(key, 22), (shards, N_LEAF), 0, OWN).astype(jnp.int32)
    slot = jnp.arange(NA, dtype=jnp.int32)
    owners = orders[:, slot % N_LEAF]
    local_block = (jnp.take_along_axis(offsets, owners, axis=1) + slot[None, :] // N_LEAF) % OWN
    return (owners * OWN + local_block).astype(jnp.int32)


def draw_anc_count(key, part):
    shards = N_DP * N_LEAF
    counts = jax.random.randint(jax.random.fold_in(key, 31), (shards,), 3 * NA // 4, NA + 1).astype(jnp.int32)
    chosen = jax.random.randint(jax.random.fold_in(key, 32), (N_DP,), 0, N_LEAF).astype(jnp.int32)
    index = jnp.arange(shards, dtype=jnp.int32)
    full_slot = index % N_LEAF == chosen[index // N_LEAF]
    return jnp.where(full_slot, NA, counts).astype(jnp.int32)


def raised(array, key, source, target, parts, factor):
    owner, partner = [(jnp.arange(array.shape[axis_at]) // (array.shape[axis_at] // parts)).reshape([-1 if axis == axis_at else 1 for axis in range(array.ndim)]) for axis_at in (source, target)]
    chosen = jax.random.permutation(key, parts)[partner]
    strong = (owner == chosen) | (owner == (partner + parts // 2) % parts)
    return jnp.where(strong, factor * array, array)


def block_scale(rng, extent, cuts, least, largest):
    def one(axis_at, blocks):
        heights = jax.random.uniform(jax.random.fold_in(jax.random.fold_in(rng, 6), axis_at), (blocks,), jnp.float32, least / len(cuts), largest / len(cuts))
        return jnp.repeat(jnp.exp(heights), extent[axis_at] // blocks).reshape((-1,) + (1,) * (len(extent) - axis_at - 1))

    loudness = one(*cuts[0])
    for cut in cuts[1:]:
        loudness = loudness * one(*cut)
    return loudness


def centred(own_key, dims, width, most, cuts=(), kind=jnp.bfloat16):
    array = jax.random.normal(own_key, dims, jnp.float32) * width
    if len(cuts) > 0:
        array = block_scale(own_key, dims, cuts, -0.22, 0.18) * array
    return jnp.clip(array, min=-most, max=most).astype(kind)


def heavy_noise(stream_key, extent, deviation, reach, cuts, heavy, held_as=jnp.bfloat16):
    result = deviation * jax.random.normal(stream_key, extent, jnp.float32)
    if cuts:
        result = result * block_scale(stream_key, extent, cuts, -0.22, 0.18)
    return jnp.clip(raised(result, jax.random.fold_in(stream_key, 3), *heavy), -reach, reach).astype(held_as)


def setup_inputs(seed: int = 0) -> dict:
    key_of = jax.random.split(jax.random.key(seed), 11)
    return {
        "queries": draw_queries(jax.random.fold_in(key_of[10], 71), 0),
        "branch_keys": draw_branch_keys(jax.random.fold_in(key_of[10], 71), 0),
        "branch_value_rows": centred(key_of[2], (N_DP * N_LEAF * BRANCH_TOKENS, KEY_VALUE_HEADS * HEAD_SIZE), 1.0, 6.0, ((0, 128),)),
        "attention_output": centred(key_of[3], (N_DP * N_LEAF * BRANCH_TOKENS, QUERY_HEADS * HEAD_SIZE), 0.3, 1.75, ((0, 128),)),
        "output_gradient": centred(key_of[4], (N_DP * N_LEAF * BRANCH_TOKENS, QUERY_HEADS * HEAD_SIZE), 16.0, 96.0, ((0, 128),)),
        "anc_states": heavy_noise(key_of[5], (N_DP * N_LEAF * OWN * BLK, MODEL_WIDTH), 1.0, 24.0, ((0, 128),), (0, 1, 128, 5.5)),
        "key_matrix": centred(key_of[6], (MODEL_WIDTH, KEY_VALUE_HEADS * HEAD_SIZE), MODEL_WIDTH ** -0.5, 0.09375),
        "value_matrix": centred(key_of[7], (MODEL_WIDTH, KEY_VALUE_HEADS * HEAD_SIZE), MODEL_WIDTH ** -0.5, 0.09375),
        "anc_blocks": draw_anc_blocks(jax.random.fold_in(key_of[10], 71), 0),
        "anc_count": draw_anc_count(jax.random.fold_in(key_of[10], 71), 0),
    }


def attend(queries, key_tokens, values, attention_output, output_gradient, key_live):
    group_width = QUERY_HEADS // KEY_VALUE_HEADS
    query_tokens = queries.shape[0]
    key_count = key_tokens.shape[0]
    anc_keys = key_count - query_tokens
    score_scale = 1.0 / math.sqrt(HEAD_SIZE)
    row_tok = jnp.arange(query_tokens * group_width, dtype=jnp.int32) // group_width
    key_pos = jnp.arange(key_count, dtype=jnp.int32)
    causal = key_pos[None, :] - anc_keys <= row_tok[:, None]
    visible = jnp.where(key_pos[None, :] < anc_keys, key_live[None, :], causal)
    query_head_rows = queries.reshape(query_tokens, KEY_VALUE_HEADS, group_width * HEAD_SIZE)
    output_heads = attention_output.reshape(query_tokens, KEY_VALUE_HEADS, group_width * HEAD_SIZE)
    head_gradients = output_gradient.reshape(query_tokens, KEY_VALUE_HEADS, group_width * HEAD_SIZE)
    query_parts, key_parts, value_parts = ([], [], [])
    for key_value_head in range(KEY_VALUE_HEADS):
        query_block = query_head_rows[:, key_value_head].reshape(query_tokens * group_width, HEAD_SIZE)
        out_block = output_heads[:, key_value_head].reshape(query_tokens * group_width, HEAD_SIZE)
        grad_block = head_gradients[:, key_value_head].reshape(query_tokens * group_width, HEAD_SIZE)
        key_block = key_tokens[:, key_value_head * HEAD_SIZE:(key_value_head + 1) * HEAD_SIZE]
        value_block = values[:, key_value_head * HEAD_SIZE:(key_value_head + 1) * HEAD_SIZE]
        scores = jnp.dot(query_block, key_block.T, preferred_element_type=jnp.float32) * score_scale
        scores = jnp.where(visible, scores, -1e+30)
        row_max = lax.optimization_barrier(jnp.max(scores, axis=1, keepdims=True))
        weights = jnp.exp(scores - row_max)
        attn_probs = weights / lax.optimization_barrier(jnp.sum(weights, axis=1, keepdims=True))
        probs_b = attn_probs.astype(jnp.bfloat16)
        dprobs = jnp.dot(grad_block, value_block.T, preferred_element_type=jnp.float32)
        row_delta = lax.optimization_barrier(jnp.sum(grad_block.astype(jnp.float32) * out_block.astype(jnp.float32), axis=1, keepdims=True))
        dscores = (attn_probs * (dprobs - row_delta)).astype(jnp.bfloat16)
        grad_query = jnp.dot(dscores, key_block, preferred_element_type=jnp.float32) * score_scale
        grad_key = jnp.dot(dscores.T, query_block, preferred_element_type=jnp.float32) * score_scale
        grad_value = jnp.dot(probs_b.T, grad_block, preferred_element_type=jnp.float32)
        query_parts.append(grad_query.reshape(query_tokens, group_width * HEAD_SIZE))
        key_parts.append(grad_key)
        value_parts.append(grad_value)
    query_grad = jnp.concatenate(query_parts, axis=1).astype(jnp.bfloat16)
    kv_partial = jnp.concatenate(key_parts + value_parts, axis=1).astype(jnp.bfloat16)
    return (query_grad, kv_partial)

def reference(queries, branch_keys, branch_value_rows, attention_output, output_gradient, anc_states, key_matrix, value_matrix, anc_blocks, anc_count):
    shards = N_DP * N_LEAF
    key_value_width = KEY_VALUE_HEADS * HEAD_SIZE
    kv_weight = jnp.concatenate([key_matrix, value_matrix], axis=1)
    kv_pool = jnp.dot(anc_states, kv_weight, preferred_element_type=jnp.float32).astype(jnp.bfloat16)
    kv_pool = kv_pool.reshape(shards * OWN, BLK, 2 * key_value_width)
    group_base = jnp.arange(shards, dtype=jnp.int32) // N_LEAF * (N_LEAF * OWN)
    slot_ids = (anc_blocks + group_base[:, None]).astype(jnp.int32)

    def one_device(inputs):
        query_tokens, key_rows, value_rows, out_rows, grad_rows, block_ids, live_count = inputs
        slot_kv = kv_pool[block_ids].reshape(NA * BLK, 2 * key_value_width)
        key_tokens = jnp.concatenate([slot_kv[:, :key_value_width], key_rows], axis=0)
        values = jnp.concatenate([slot_kv[:, key_value_width:], value_rows], axis=0)
        live_slot = jnp.arange(NA, dtype=jnp.int32) < live_count
        key_live = jnp.concatenate([jnp.repeat(live_slot, BLK), jnp.ones((BRANCH_TOKENS,), dtype=bool)])
        query_grad, kv_partial = attend(query_tokens, key_tokens, values, out_rows, grad_rows, key_live)
        branch_part = kv_partial[NA * BLK:]
        slot_part = kv_partial[:NA * BLK].reshape(NA, BLK, 2 * key_value_width)
        return (query_grad, branch_part[:, :key_value_width], branch_part[:, key_value_width:], slot_part)
    inputs = (queries.reshape(shards, BRANCH_TOKENS, QUERY_HEADS * HEAD_SIZE), branch_keys.reshape(shards, BRANCH_TOKENS, key_value_width), branch_value_rows.reshape(shards, BRANCH_TOKENS, key_value_width), attention_output.reshape(shards, BRANCH_TOKENS, QUERY_HEADS * HEAD_SIZE), output_gradient.reshape(shards, BRANCH_TOKENS, QUERY_HEADS * HEAD_SIZE), slot_ids, anc_count)
    query_grad, key_grad, value_grad, slot_grads = lax.map(one_device, inputs)
    live_all = (jnp.arange(NA, dtype=jnp.int32)[None, :] < anc_count[:, None]).astype(jnp.float32)
    terms = slot_grads.astype(jnp.float32) * live_all[:, :, None, None]
    totals = jnp.zeros((shards * OWN, BLK, 2 * key_value_width), jnp.float32)
    totals = totals.at[slot_ids.reshape(-1)].add(terms.reshape(shards * NA, BLK, 2 * key_value_width))
    kv_total = totals.astype(jnp.bfloat16).reshape(shards * OWN * BLK, 2 * key_value_width)
    anc_state_grad = jnp.dot(kv_total, kv_weight.T, preferred_element_type=jnp.float32).astype(jnp.bfloat16)
    weight_grad = jnp.dot(anc_states.T, kv_total, preferred_element_type=jnp.float32) / shards
    return (query_grad.reshape(shards * BRANCH_TOKENS, QUERY_HEADS * HEAD_SIZE), key_grad.reshape(shards * BRANCH_TOKENS, key_value_width), value_grad.reshape(shards * BRANCH_TOKENS, key_value_width), anc_state_grad, weight_grad[:, :key_value_width], weight_grad[:, key_value_width:])
```

```python
import functools
import math

import jax
import jax.numpy as jnp
from jax import lax
from jax.experimental import pallas as pl
from jax.experimental.pallas import tpu as pltpu
from jax.sharding import PartitionSpec as P

BF = jnp.bfloat16
F32 = jnp.float32
WIDTH = 3584
HEADS = 4
GROUP = 7
HEAD = 128
NA = 16
BLK = 64
TOK = 256
ANC = NA * BLK
KEYS = ANC + TOK
OWN = 128
COLS = WIDTH // 4
SCALE = 1.0 / math.sqrt(HEAD)
EXP2_SCALE = SCALE * math.log2(math.e)
NEG = -1e30
MIB = 1024 * 1024


def contract_rows(left, right):
    return lax.dot_general(left, right, (((0,), (0,)), ((), ())), preferred_element_type=F32)


def contract_cols(left, right):
    return lax.dot_general(left, right, (((1,), (1,)), ((), ())), preferred_element_type=F32)


def wrap(v):
    return lax.rem(v + 4, 4)


class Place:
    def __init__(self):
        leaf = lax.axis_index("leaf")
        self.g = lax.axis_index("dp")
        self.leaf = leaf
        self.c = lax.rem(leaf, 2)
        y = lax.rem(lax.div(leaf, 2), 4)
        z = lax.div(leaf, 8)
        self.a = z + self.c * (y - z)
        self.b = y + self.c * (z - y)

    def chip(self, a, b):
        return a * 4 + b + self.c * (3 * b - 3 * a)

    def at(self, a, b):
        return (self.g, self.chip(a, b) * 2 + self.c)

    def sibling(self):
        return (self.g, self.leaf + 1 - 2 * self.c)

    def along_x(self, d):
        return (wrap(self.g + d), self.leaf)

    def ring(self):
        return {
            "b+": self.at(self.a, wrap(self.b + 1)),
            "b-": self.at(self.a, wrap(self.b - 1)),
            "a+": self.at(wrap(self.a + 1), self.b),
            "a-": self.at(wrap(self.a - 1), self.b),
        }


def send(src, dst, ssem, rsem, to):
    copy = pltpu.make_async_remote_copy(
        src_ref=src,
        dst_ref=dst,
        send_sem=ssem,
        recv_sem=rsem,
        device_id=to,
        device_id_type=pl.DeviceIdType.MESH,
    )
    copy.start()
    return copy


def greet(me):
    barrier = pltpu.get_barrier_semaphore()
    others = list(me.ring().values()) + [me.sibling()] + [me.along_x(d) for d in (1, 2, 3)]
    for other in others:
        pl.semaphore_signal(barrier, inc=1, device_id=other, device_id_type=pl.DeviceIdType.MESH)
    pl.semaphore_wait(barrier, len(others))


def gather_kernel(
    anc_hbm, wk_hbm, wv_hbm, kvg_out, ancx_out,
    anc, wk, wv, own, kvg0, kvg1, kvg2, kvg3, ancx, lsem, osem, ssem, rsem, xssem, xrsem,
):
    me = Place()
    c, a, b = me.c, me.a, me.b
    kvg = [kvg0, kvg1, kvg2, kvg3]
    loads = [
        pltpu.make_async_copy(anc_hbm, anc, lsem.at[0]),
        pltpu.make_async_copy(wk_hbm, wk, lsem.at[1]),
        pltpu.make_async_copy(wv_hbm, wv, lsem.at[2]),
    ]
    for load in loads:
        load.start()
    greet(me)
    ring = me.ring()
    ab, bb = wrap(a + 1), wrap(a - 1)
    sib = me.sibling()
    away = []
    for d in (1, 2, 3):
        cols = pl.ds(pl.multiple_of(wrap(me.g + d) * COLS, 128), COLS)
        away.append(
            send(anc_hbm.at[:, cols], ancx.at[me.g, c], xssem.at[d], xrsem.at[d], me.along_x(d))
        )
    loads[0].wait()
    mine = pl.ds(pl.multiple_of(me.g * COLS, 128), COLS)
    ancx[me.g, c] = anc[:, mine]
    for t, (w, load) in enumerate(((wk, loads[1]), (wv, loads[2]))):
        load.wait()
        kv = jnp.dot(anc[...], w[...], preferred_element_type=F32).astype(BF)
        for h in range(HEADS):
            own[t, h] = kv[:, h * HEAD : (h + 1) * HEAD]
    copies = [{} for _ in range(HEADS)]

    def go(h, k, src, dst, to):
        copies[h][k] = send(src, dst, ssem.at[h, k], rsem.at[h, k], to)

    for h in range(HEADS):
        go(h, 0, own.at[1 - c, h], kvg[h].at[1 - c, b, a, c], sib)
        kvg[h][c, a, b, c] = own[c, h]
    for h in range(HEADS):
        copies[h][0].wait_recv()
        here = kvg[h].at[c, a, b]
        go(h, 1, here, here, ring["b+"])
        go(h, 2, here, here, ring["b-"])
    for h in range(HEADS):
        copies[h][1].wait_recv()
        half = kvg[h].at[c, a, wrap(b - 1), 0]
        go(h, 3, half, half, ring["b+"])
        copies[h][2].wait_recv()
        half = kvg[h].at[c, a, wrap(b + 1), 1]
        go(h, 4, half, half, ring["b-"])
    for h in range(HEADS):
        copies[h][3].wait_recv()
        copies[h][4].wait_recv()
        row = kvg[h].at[c, a]
        go(h, 5, row, row, ring["a+"])
        go(h, 6, row, row, ring["a-"])
        go(h, 9, row, row, sib)
    sent_x = []
    sent_x.append(send(ancx.at[me.g, c], ancx.at[me.g, c], xssem.at[4], xrsem.at[4], sib))
    for d in (1, 2, 3):
        away[d - 1].wait_recv()
        part = ancx.at[wrap(me.g - d), c]
        sent_x.append(send(part, part, xssem.at[4 + d], xrsem.at[4 + d], sib))
    for h in range(HEADS):
        copies[h][5].wait_recv()
        half = kvg[h].at[c, wrap(a - 1), pl.ds(0, 2)]
        go(h, 7, half, half, ring["a+"])
        row = kvg[h].at[c, wrap(a - 1)]
        go(h, 10, row, row, sib)
        copies[h][6].wait_recv()
        half = kvg[h].at[c, wrap(a + 1), pl.ds(2, 2)]
        go(h, 8, half, half, ring["a-"])
        row = kvg[h].at[c, wrap(a + 1)]
        go(h, 11, row, row, sib)
    for h in range(HEADS):
        copies[h][7].wait_recv()
        copies[h][8].wait_recv()
        row = kvg[h].at[c, wrap(a + 2)]
        go(h, 12, row, row, sib)
    for copy in sent_x:
        copy.wait_recv()
    outs = [pltpu.make_async_copy(ancx, ancx_out, osem.at[HEADS])]
    outs[0].start()
    for h in range(HEADS):
        for k in (9, 10, 11, 12):
            copies[h][k].wait_recv()
        out = pltpu.make_async_copy(kvg[h], kvg_out.at[h], osem.at[h])
        out.start()
        outs.append(out)
    for h in range(HEADS):
        for k in range(13):
            copies[h][k].wait_send()
    for copy in away + sent_x:
        copy.wait_send()
    for out in outs:
        out.wait()


def gather_call(anc, wk, wv):
    hbm = pl.BlockSpec(memory_space=pl.ANY)
    kvg = pltpu.VMEM((2, 4, 4, 2, OWN, HEAD), BF)
    return pl.pallas_call(
        gather_kernel,
        out_shape=(
            jax.ShapeDtypeStruct((HEADS, 2, 4, 4, 2, OWN, HEAD), BF),
            jax.ShapeDtypeStruct((4, 2, OWN, COLS), BF),
        ),
        in_specs=[hbm] * 3,
        out_specs=(hbm, hbm),
        scratch_shapes=[
            pltpu.VMEM((OWN, WIDTH), BF),
            pltpu.VMEM((WIDTH, HEADS * HEAD), BF),
            pltpu.VMEM((WIDTH, HEADS * HEAD), BF),
            pltpu.VMEM((2, HEADS, OWN, HEAD), BF),
            kvg, kvg, kvg, kvg,
            pltpu.VMEM((4, 2, OWN, COLS), BF),
            pltpu.SemaphoreType.DMA((3,)),
            pltpu.SemaphoreType.DMA((HEADS + 1,)),
            pltpu.SemaphoreType.DMA((HEADS, 13)),
            pltpu.SemaphoreType.DMA((HEADS, 13)),
            pltpu.SemaphoreType.DMA((8,)),
            pltpu.SemaphoreType.DMA((8,)),
        ],
        compiler_params=pltpu.CompilerParams(
            collective_id=0, has_side_effects=True, vmem_limit_bytes=56 * MIB
        ),
        name="gather_kv",
    )(anc, wk, wv)


def attend_kernel(
    blocks, count, kvg, q, out, grad, bk, bv, dq_out, slots_out, dbk_out, dbv_out,
    ks, vs, kt, s, dk, dv,
):
    for j in range(NA):
        blk = blocks[0, j]
        leaf = lax.div(blk, 2)
        z, y, d = lax.div(leaf, 8), lax.rem(lax.div(leaf, 2), 4), lax.rem(leaf, 2)
        part = lax.rem(blk, 2)
        rows = pl.ds(j * BLK, BLK)
        ks[rows] = kvg[0, 0, ((z * 4 + y) * 2 + d) * 2 + part]
        vs[rows] = kvg[0, 1, ((y * 4 + z) * 2 + d) * 2 + part]
    ks[pl.ds(ANC, TOK)] = bk[...]
    vs[pl.ds(ANC, TOK)] = bv[...]
    kt[...] = ks[...].T
    dk[...] = jnp.zeros_like(dk)
    dv[...] = jnp.zeros_like(dv)
    live = [j < count[0] for j in range(NA)]
    ones = jnp.ones((8, HEAD), BF)

    def one(h, carry):
        cols = pl.ds(pl.multiple_of(h * HEAD, HEAD), HEAD)
        qh = q[:, cols]
        gh = grad[:, cols]
        prod = gh.astype(F32) * out[:, cols].astype(F32)
        hi = prod.astype(BF)
        lo = (prod - hi.astype(F32)).astype(BF)
        delta = (contract_cols(ones, hi) + contract_cols(ones, lo))[0:1]
        top = jnp.full((8, TOK), NEG, F32)
        for ch in range(4):
            sc = contract_cols(ks[pl.ds(ch * 256, 256)], qh)
            s[pl.ds(ch * 256, 256)] = sc
            for j in range(4):
                part = sc[j * BLK : (j + 1) * BLK].reshape(8, 8, TOK).max(axis=0)
                top = jnp.maximum(top, jnp.where(live[ch * 4 + j], part, NEG))
        sc = contract_cols(ks[pl.ds(ANC, TOK)], qh)
        seen = lax.broadcasted_iota(jnp.int32, (TOK, TOK), 0) <= lax.broadcasted_iota(
            jnp.int32, (TOK, TOK), 1
        )
        sc = jnp.where(seen, sc, NEG)
        s[pl.ds(ANC, TOK)] = sc
        top = jnp.maximum(top, sc.reshape(32, 8, TOK).max(axis=0))
        top = top.max(axis=0, keepdims=True) * EXP2_SCALE
        total = jnp.zeros((8, TOK), F32)
        for j in range(NA):
            rows = pl.ds(j * BLK, BLK)
            e = jnp.exp2(s[rows] * EXP2_SCALE - jnp.where(live[j], top, 1e30))
            s[rows] = e
            total = total + e.reshape(8, 8, TOK).sum(axis=0)
        rows = pl.ds(ANC, TOK)
        e = jnp.exp2(s[rows] * EXP2_SCALE - top)
        s[rows] = e
        total = total + e.reshape(32, 8, TOK).sum(axis=0)
        inv = 1.0 / total.sum(axis=0, keepdims=True)
        dqt = jnp.zeros((HEAD, TOK), F32)
        for ch in range(5):
            rows = pl.ds(ch * 256, 256)
            p = s[rows] * inv
            dp = contract_cols(vs[rows], gh)
            ds = (p * (dp - delta)).astype(BF)
            dv[rows] += jnp.dot(p.astype(BF), gh, preferred_element_type=F32)
            dk[rows] += jnp.dot(ds, qh, preferred_element_type=F32)
            dqt = dqt + jnp.dot(kt[:, ch * 256 : (ch + 1) * 256], ds, preferred_element_type=F32)
        dq_out[:, cols] = (dqt * SCALE).T.astype(BF)
        return carry

    lax.fori_loop(0, GROUP, one, 0)
    slots_out[0, 0] = (dk[pl.ds(0, ANC)] * SCALE).astype(BF)
    slots_out[0, 1] = dv[pl.ds(0, ANC)].astype(BF)
    dbk_out[...] = (dk[pl.ds(ANC, TOK)] * SCALE).astype(BF)
    dbv_out[...] = dv[pl.ds(ANC, TOK)].astype(BF)


def attend_call(blocks, count, kvg, q, out, grad, bk, bv):
    smem = pl.BlockSpec(memory_space=pltpu.SMEM)
    wide = pl.BlockSpec((TOK, GROUP * HEAD), lambda h: (0, h))
    narrow = pl.BlockSpec((TOK, HEAD), lambda h: (0, h))
    return pl.pallas_call(
        attend_kernel,
        grid=(HEADS,),
        out_shape=(
            jax.ShapeDtypeStruct((TOK, WIDTH), BF),
            jax.ShapeDtypeStruct((HEADS, 2, ANC, HEAD), BF),
            jax.ShapeDtypeStruct((TOK, HEADS * HEAD), BF),
            jax.ShapeDtypeStruct((TOK, HEADS * HEAD), BF),
        ),
        in_specs=[
            smem,
            smem,
            pl.BlockSpec((1, 2, 64, BLK, HEAD), lambda h: (h, 0, 0, 0, 0)),
            wide,
            wide,
            wide,
            narrow,
            narrow,
        ],
        out_specs=(
            wide,
            pl.BlockSpec((1, 2, ANC, HEAD), lambda h: (h, 0, 0, 0)),
            narrow,
            narrow,
        ),
        scratch_shapes=[
            pltpu.VMEM((KEYS, HEAD), BF),
            pltpu.VMEM((KEYS, HEAD), BF),
            pltpu.VMEM((HEAD, KEYS), BF),
            pltpu.VMEM((KEYS, TOK), F32),
            pltpu.VMEM((KEYS, HEAD), F32),
            pltpu.VMEM((KEYS, HEAD), F32),
        ],
        compiler_params=pltpu.CompilerParams(vmem_limit_bytes=48 * MIB),
        name="attend",
    )(blocks, count, kvg.reshape(HEADS, 2, 64, BLK, HEAD), q, out, grad, bk, bv)


def add(x, y):
    return (x.astype(F32) + y.astype(F32)).astype(BF)


class Scatter:
    def __init__(self, me, data, first, full, edge, edge_first, edge_full, ssem, rsem):
        self.me, self.data, self.first, self.full = me, data, first, full
        self.edge, self.edge_first, self.edge_full = edge, edge_first, edge_full
        self.ssem, self.rsem = ssem, rsem
        self.copies = {}

    def go(self, k, src, dst, to):
        self.copies[k] = send(src, dst, self.ssem(k), self.rsem(k), self.me.ring()[to])

    def step(self, n):
        me, data = self.me, self.data
        up, down, far = wrap(me.a + 1), wrap(me.a - 1), wrap(me.a + 2)
        right, left, off = wrap(me.b + 1), wrap(me.b - 1), wrap(me.b + 2)
        copies = self.copies
        if n == 0:
            self.go(0, data.at[far, pl.ds(0, 2)], self.first.at[0], "a+")
            self.go(1, data.at[far, pl.ds(2, 2)], self.first.at[1], "a-")
        elif n == 1:
            copies[0].wait_recv()
            data[up, pl.ds(0, 2)] = add(data[up, pl.ds(0, 2)], self.first[0])
            self.go(2, data.at[up], self.full.at[0], "a+")
            copies[1].wait_recv()
            data[down, pl.ds(2, 2)] = add(data[down, pl.ds(2, 2)], self.first[1])
            self.go(3, data.at[down], self.full.at[1], "a-")
        elif n == 2:
            copies[2].wait_recv()
            copies[3].wait_recv()
            for j in range(4):
                b = wrap(me.b + (2, 1, 3, 0)[j])
                total = data[me.a, b].astype(F32) + self.full[0, b].astype(F32)
                self.edge[b] = (total + self.full[1, b].astype(F32)).astype(BF)
                if j == 0:
                    self.go(4, self.edge.at[off, 0], self.edge_first.at[0], "b+")
                    self.go(5, self.edge.at[off, 1], self.edge_first.at[1], "b-")
        elif n == 3:
            copies[4].wait_recv()
            self.edge[right, 0] = add(self.edge[right, 0], self.edge_first[0])
            self.go(6, self.edge.at[right], self.edge_full.at[0], "b+")
            copies[5].wait_recv()
            self.edge[left, 1] = add(self.edge[left, 1], self.edge_first[1])
            self.go(7, self.edge.at[left], self.edge_full.at[1], "b-")
        else:
            copies[6].wait_recv()
            copies[7].wait_recv()
            total = self.edge[me.b].astype(F32) + self.edge_full[0].astype(F32)
            return total + self.edge_full[1].astype(F32)

    def finish(self):
        for copy in self.copies.values():
            copy.wait_send()


def reduce_kernel(
    own_code, sib_code, slots, ancx, wk_hbm, wv_hbm, dstate_out, gk_out, gv_out,
    wk, wv, sib0, sib1, sib2, sib3, dense, first, full, edge, edge_first, edge_full,
    tot, pair, xt0, xt1, xt2, xt3, part, part_bf, wfirst, wfull, wedge, wedge_first, wedge_full,
    fin, fin_in, lsem, sibs, sibr, rss, rsr, prs, prr, xs, xr, ws, wr, fs, fr,
):
    me = Place()
    c = me.c
    sib = [sib0, sib1, sib2, sib3]
    xt = [xt0, xt1, xt2, xt3]
    loads = [
        pltpu.make_async_copy(wk_hbm, wk, lsem.at[0]),
        pltpu.make_async_copy(wv_hbm, wv, lsem.at[1]),
    ]
    for load in loads:
        load.start()
    greet(me)
    over = [send(slots.at[h, 1 - c], sib[h], sibs.at[h], sibr.at[h], me.sibling()) for h in range(HEADS)]
    runs = []
    for h in range(HEADS):
        run = Scatter(
            me, dense.at[h], first.at[h], full.at[h], edge.at[h], edge_first.at[h], edge_full.at[h],
            functools.partial(lambda h, k: rss.at[h, k], h),
            functools.partial(lambda h, k: rsr.at[h, k], h),
        )
        over[h].wait_recv()
        for i in (2, 1, 3, 0):
            row = wrap(me.a + i)
            for j in range(4):
                for d in range(2):
                    o = me.chip(row, j) * 2 + d
                    mine, theirs = own_code[o], sib_code[o]
                    slot = lax.div(mine, 4)
                    x = slots[h, c, slot]
                    slot = lax.div(theirs, 4)
                    y = sib[h][slot]
                    for block in range(2):
                        dense[h, row, j, d, pl.ds(block * BLK, BLK)] = add(
                            jnp.where(lax.rem(mine, 4) == block + 1, x, 0),
                            jnp.where(lax.rem(theirs, 4) == block + 1, y, 0),
                        )
            if i == 2:
                run.step(0)
        runs.append(run)
    for h in range(HEADS):
        runs[h].step(1)
    for h in range(HEADS):
        runs[h].step(2)
    for h in range(HEADS):
        runs[h].step(3)
    pairs, across, passed = [], [], []
    for h in range(HEADS):
        total = runs[h].step(4).astype(BF)
        tot[h] = total
        xt[h][me.g] = total
        pairs.append(send(tot.at[h, 1 - c], pair.at[h], prs.at[h], prr.at[h], me.sibling()))
        here = xt[h].at[me.g]
        across.append(
            [
                send(tot.at[h], here, xs.at[h, 0], xr.at[h, 0], me.along_x(1)),
                send(tot.at[h], here, xs.at[h, 1], xr.at[h, 1], me.along_x(-1)),
            ]
        )
    for h in range(HEADS):
        across[h][0].wait_recv()
        half = xt[h].at[wrap(me.g - 1), 0]
        passed.append(send(half, half, xs.at[h, 2], xr.at[h, 2], me.along_x(1)))
        across[h][1].wait_recv()
        half = xt[h].at[wrap(me.g + 1), 1]
        passed.append(send(half, half, xs.at[h, 3], xr.at[h, 3], me.along_x(-1)))
    for load in loads:
        load.wait()
    for h in range(HEADS):
        pairs[h].wait_recv()
    first_cols, last_cols = [], []
    for h in range(HEADS):
        mine, other = tot[h, c], pair[h]
        first_cols.append(jnp.where(c == 0, mine, other))
        last_cols.append(jnp.where(c == 0, other, mine))
    first_cols = jnp.concatenate(first_cols, axis=1)
    last_cols = jnp.concatenate(last_cols, axis=1)
    for n in range(0, WIDTH, 512):
        grad = contract_cols(first_cols, wk[pl.ds(n, 512)])
        grad = grad + contract_cols(last_cols, wv[pl.ds(n, 512)])
        dstate_out[:, pl.ds(n, 512)] = grad.astype(BF)
    for copy in passed:
        copy.wait_recv()
    totals = jnp.concatenate([xt[h][...].reshape(1024, HEAD) for h in range(HEADS)], axis=1)
    part[...] = contract_rows(ancx[...].reshape(1024, COLS), totals).reshape(16, 56, 512)
    run = Scatter(
        me, part_bf, wfirst, wfull, wedge, wedge_first, wedge_full,
        lambda k: ws.at[k], lambda k: wr.at[k],
    )
    for i in (2, 1, 3, 0):
        row = wrap(me.a + i)
        for j in range(4):
            x = part[me.chip(row, j)]
            x = jnp.concatenate([x, jnp.zeros((8, 512), F32)], axis=0).astype(BF)
            part_bf[row, j, 0] = x[:, :256]
            part_bf[row, j, 1] = x[:, 256:]
        if i == 2:
            run.step(0)
    for n in (1, 2, 3):
        run.step(n)
    done = run.step(4) * (1.0 / 128.0)
    fin[...] = done
    last = send(fin, fin_in, fs.at[0], fr.at[0], me.sibling())

    def rows_of(ref):
        both = jnp.concatenate([ref[0], ref[1]], axis=1)
        return jnp.where(c == 0, both[0:28], both[28:56])

    own = rows_of(fin)
    last.wait_recv()
    other = rows_of(fin_in)
    gk_out[...] = jnp.where(c == 0, own, other)
    gv_out[...] = jnp.where(c == 0, other, own)
    for run_ in runs + [run]:
        run_.finish()
    for copy in over + pairs + passed + [last] + [x for two in across for x in two]:
        copy.wait_send()


def reduce_call(own_code, sib_code, slots, ancx, wk, wv):
    hbm = pl.BlockSpec(memory_space=pl.ANY)
    smem = pl.BlockSpec(memory_space=pltpu.SMEM)
    vmem = pl.BlockSpec(memory_space=pltpu.VMEM)
    dma = pltpu.SemaphoreType.DMA
    sib = pltpu.VMEM((NA, BLK, HEAD), BF)
    xt = pltpu.VMEM((4, 2, OWN, HEAD), BF)
    return pl.pallas_call(
        reduce_kernel,
        out_shape=(
            jax.ShapeDtypeStruct((OWN, WIDTH), BF),
            jax.ShapeDtypeStruct((28, 512), F32),
            jax.ShapeDtypeStruct((28, 512), F32),
        ),
        in_specs=[smem, smem, vmem, vmem, hbm, hbm],
        out_specs=(vmem, vmem, vmem),
        scratch_shapes=[
            pltpu.VMEM((WIDTH, HEADS * HEAD), BF),
            pltpu.VMEM((WIDTH, HEADS * HEAD), BF),
            sib, sib, sib, sib,
            pltpu.VMEM((HEADS, 4, 4, 2, OWN, HEAD), BF),
            pltpu.VMEM((HEADS, 2, 2, 2, OWN, HEAD), BF),
            pltpu.VMEM((HEADS, 2, 4, 2, OWN, HEAD), BF),
            pltpu.VMEM((HEADS, 4, 2, OWN, HEAD), BF),
            pltpu.VMEM((HEADS, 2, OWN, HEAD), BF),
            pltpu.VMEM((HEADS, 2, 2, OWN, HEAD), BF),
            pltpu.VMEM((HEADS, 2, OWN, HEAD), BF),
            pltpu.VMEM((HEADS, OWN, HEAD), BF),
            xt, xt, xt, xt,
            pltpu.VMEM((16, 56, 512), F32),
            pltpu.VMEM((4, 4, 2, 64, 256), BF),
            pltpu.VMEM((2, 2, 2, 64, 256), BF),
            pltpu.VMEM((2, 4, 2, 64, 256), BF),
            pltpu.VMEM((4, 2, 64, 256), BF),
            pltpu.VMEM((2, 64, 256), BF),
            pltpu.VMEM((2, 2, 64, 256), BF),
            pltpu.VMEM((2, 64, 256), F32),
            pltpu.VMEM((2, 64, 256), F32),
            dma((2,)),
            dma((HEADS,)), dma((HEADS,)),
            dma((HEADS, 8)), dma((HEADS, 8)),
            dma((HEADS,)), dma((HEADS,)),
            dma((HEADS, 4)), dma((HEADS, 4)),
            dma((8,)), dma((8,)),
            dma((1,)), dma((1,)),
        ],
        compiler_params=pltpu.CompilerParams(
            collective_id=1, has_side_effects=True, vmem_limit_bytes=56 * MIB
        ),
        name="reduce_kv",
    )(own_code, sib_code, slots.reshape(HEADS, 2, NA, BLK, HEAD), ancx, wk, wv)


def on_device(q, bk, bv, out, grad, anc, wk, wv, blocks, count):
    slot = jnp.arange(NA, dtype=jnp.int32)
    leaves = jnp.arange(32, dtype=jnp.int32)
    code = jnp.where(
        (blocks[0][:, None] // 2 == leaves[None, :]) & (slot < count[0])[:, None],
        slot[:, None] * 4 + blocks[0][:, None] % 2 + 1,
        0,
    ).sum(axis=0, dtype=jnp.int32)
    sib_code = lax.ppermute(code, "leaf", [(i, i ^ 1) for i in range(32)])
    kvg, ancx = gather_call(anc, wk, wv)
    dq, slots, dbk, dbv = attend_call(blocks, count, kvg, q, out, grad, bk, bv)
    dstate, gk, gv = reduce_call(code, sib_code, slots, ancx, wk, wv)
    return dq, dbk, dbv, dstate, gk, gv


def solution(mesh):
    rows = P(("dp", "leaf"), None)
    return jax.shard_map(
        on_device,
        mesh=mesh,
        in_specs=(rows, rows, rows, rows, rows, rows, P(), P(), rows, P(("dp", "leaf"))),
        out_specs=(rows,) * 6,
        check_vma=False,
    )
```

```python
import functools
import math

import jax
import jax.numpy as jnp
from jax import lax
from jax.experimental import pallas as pl
from jax.experimental.pallas import tpu as pltpu
from jax.sharding import PartitionSpec as P

BF = jnp.bfloat16
F32 = jnp.float32
WIDTH = 3584
HEADS = 4
GROUP = 7
HEAD = 128
NA = 16
BLK = 64
TOK = 256
ANC = NA * BLK
KEYS = ANC + TOK
OWN = 128
COLS = WIDTH // 4
SCALE = 1.0 / math.sqrt(HEAD)
EXP2_SCALE = SCALE * math.log2(math.e)
NEG = -1e30
MIB = 1024 * 1024


def contract_rows(left, right):
    return lax.dot_general(left, right, (((0,), (0,)), ((), ())), preferred_element_type=F32)


def contract_cols(left, right):
    return lax.dot_general(left, right, (((1,), (1,)), ((), ())), preferred_element_type=F32)


def wrap(v):
    return lax.rem(v + 4, 4)


class Place:
    def __init__(self):
        leaf = lax.axis_index("leaf")
        self.g = lax.axis_index("dp")
        self.leaf = leaf
        self.c = lax.rem(leaf, 2)
        self.other = 1 - self.c
        y = lax.rem(lax.div(leaf, 2), 4)
        z = lax.div(leaf, 8)
        self.a = z + self.c * (y - z)
        self.b = y + self.c * (z - y)
        self.up, self.down, self.far = (wrap(self.a + d) for d in (1, -1, 2))
        self.right, self.left, self.off = (wrap(self.b + d) for d in (1, -1, 2))
        self.next, self.last, self.over = (wrap(self.g + d) for d in (1, -1, 2))
        self.ring = {
            "b+": self.at(self.a, self.right),
            "b-": self.at(self.a, self.left),
            "a+": self.at(self.up, self.b),
            "a-": self.at(self.down, self.b),
            "a2": self.at(self.far, self.b),
            "b2": self.at(self.a, self.off),
            "x+": (self.next, leaf),
            "x-": (self.last, leaf),
            "x2": (self.over, leaf),
            "sib": (self.g, leaf + 1 - 2 * self.c),
        }

    def chip(self, a, b):
        return a * 4 + b + self.c * (3 * b - 3 * a)

    def at(self, a, b):
        return (self.g, self.chip(a, b) * 2 + self.c)


class Copy:
    def __init__(self, src, dst, ssem, rsem, to):
        self.parts = (src, dst, ssem, rsem, to)

    def make(self):
        src, dst, ssem, rsem, to = self.parts
        return pltpu.make_async_remote_copy(
            src_ref=src(),
            dst_ref=dst(),
            send_sem=ssem(),
            recv_sem=rsem(),
            device_id=to,
            device_id_type=pl.DeviceIdType.MESH,
        )

    def start(self):
        self.make().start()

    def arrive(self):
        self.make().wait_recv()

    def leave(self):
        self.make().wait_send()


def greet(me):
    barrier = pltpu.get_barrier_semaphore()
    for other in me.ring.values():
        pl.semaphore_signal(barrier, inc=1, device_id=other, device_id_type=pl.DeviceIdType.MESH)
    pl.semaphore_wait(barrier, len(me.ring))


class Flow:
    def __init__(self, me, ssem, rsem):
        self.me, self.ssem, self.rsem = me, ssem, rsem
        self.copies = {}

    def go(self, k, src, dst, to):
        copy = Copy(src, dst, lambda: self.ssem(k), lambda: self.rsem(k), self.me.ring[to])
        self.copies[k] = copy
        copy.start()

    def got(self, *ks):
        for k in ks:
            self.copies[k].arrive()

    def finish(self):
        for copy in self.copies.values():
            copy.leave()


class Gather(Flow):
    def __init__(self, me, kvg, own, ssem, rsem):
        super().__init__(me, ssem, rsem)
        self.kvg, self.own = kvg, own

    def step(self, n):
        me, kvg = self.me, self.kvg
        c, a, b = me.c, me.a, me.b
        if n == 0:
            self.go(0, lambda: self.own(me.other), lambda: kvg.at[me.other, b, a, c], "sib")
            kvg[c, a, b, c] = self.own(c)[...]
        elif n == 1:
            self.got(0)
            here = lambda: kvg.at[c, a, b]
            self.go(1, here, here, "b+")
            self.go(2, here, here, "b-")
            self.go(3, here, here, "b2")
        elif n == 2:
            self.got(1, 2, 3)
            row = lambda: kvg.at[c, a]
            self.go(5, row, row, "a+")
            self.go(6, row, row, "a-")
            self.go(9, row, row, "sib")
        elif n == 3:
            self.got(5)
            half = lambda: kvg.at[c, me.down, pl.ds(0, 2)]
            self.go(7, half, half, "a+")
            below = lambda: kvg.at[c, me.down]
            self.go(10, below, below, "sib")
            self.got(6)
            rest = lambda: kvg.at[c, me.up, pl.ds(2, 2)]
            self.go(8, rest, rest, "a-")
            above = lambda: kvg.at[c, me.up]
            self.go(11, above, above, "sib")
        elif n == 4:
            self.got(7, 8)
            far = lambda: kvg.at[c, me.far]
            self.go(12, far, far, "sib")
        else:
            self.got(9, 10, 11, 12)


def add(x, y):
    return (x.astype(F32) + y.astype(F32)).astype(BF)


class Scatter(Flow):
    def __init__(self, me, h, data, first, full, edge, edge_in, ssem, rsem):
        super().__init__(me, ssem, rsem)
        self.h = h
        self.data, self.first, self.full, self.edge, self.edge_in = data, first, full, edge, edge_in

    def spread(self, k):
        edge, edge_in, h, me = self.edge, self.edge_in, self.h, self.me
        for n, (to, b) in enumerate((("b+", me.right), ("b-", me.left), ("b2", me.off))):
            self.go(k + n, lambda b=b: edge.at[h, b], lambda n=n: edge_in.at[h, n], to)

    def total(self, k):
        self.got(k, k + 1, k + 2)
        total = self.edge[self.h, self.me.b].astype(F32)
        for n in range(3):
            total = total + self.edge_in[self.h, n].astype(F32)
        return total


class LongScatter(Scatter):
    def step(self, n):
        me, h = self.me, self.h
        data, first, full, edge = self.data, self.first, self.full, self.edge
        if n == 0:
            self.go(0, lambda: data.at[h, me.far, pl.ds(0, 2)], lambda: first.at[h, 0], "a+")
            self.go(1, lambda: data.at[h, me.far, pl.ds(2, 2)], lambda: first.at[h, 1], "a-")
        elif n == 1:
            self.got(0)
            low = pl.ds(0, 2)
            data[h, me.up, low] = add(data[h, me.up, low], first[h, 0])
            self.go(2, lambda: data.at[h, me.up], lambda: full.at[h, 0], "a+")
            self.got(1)
            high = pl.ds(2, 2)
            data[h, me.down, high] = add(data[h, me.down, high], first[h, 1])
            self.go(3, lambda: data.at[h, me.down], lambda: full.at[h, 1], "a-")
        elif n == 2:
            self.got(2, 3)
            for b in range(4):
                total = data[h, me.a, b].astype(F32) + full[h, 0, b].astype(F32)
                edge[h, b] = (total + full[h, 1, b].astype(F32)).astype(BF)
            self.spread(4)
        else:
            return self.total(4)


class ShortScatter(Scatter):
    def step(self, n):
        me, h = self.me, self.h
        data, full, edge = self.data, self.full, self.edge
        if n == 0:
            for k, (to, a) in enumerate((("a+", me.up), ("a-", me.down), ("a2", me.far))):
                self.go(k, lambda a=a: data.at[h, a], lambda k=k: full.at[h, k], to)
        elif n == 1:
            self.got(0, 1, 2)
            for b in range(4):
                total = data[h, me.a, b].astype(F32)
                for k in range(3):
                    total = total + full[h, k, b].astype(F32)
                edge[h, b] = total.astype(BF)
            self.spread(3)
        else:
            return self.total(3)


NAMES = (
    "blocks", "blocks_hbm", "count", "anc_hbm", "wk_hbm", "wv_hbm", "q_hbm", "out_hbm",
    "grad_hbm", "bk", "bv", "dq_hbm", "dbk", "dbv", "dstate_hbm", "gk", "gv", "anc", "wk", "wv",
    "q", "out", "grad", "own", "kvg0", "kvg1", "kvg2", "kvg3", "ancx", "anct", "ks", "vs", "kt",
    "eb", "btop", "bsum", "delta", "e0", "e1", "dk", "dv", "dq", "slots0", "slots1", "slots2",
    "slots3", "sib0", "sib1", "sib2", "sib3", "dense", "first", "full", "edge", "edge_in", "tot",
    "pair", "xt0", "xt1", "xt2", "xt3", "part", "wfull", "wedge", "wedge_in", "fin", "fin_in",
    "dstate", "code", "sib_code", "sib_blocks_v", "sib_blocks", "bss", "bsr", "lsem", "osem", "gss", "gsr", "ass", "asr", "rss", "rsr", "oss", "osr", "pss", "psr",
    "xss", "xsr", "wss", "wsr", "fss", "fsr",
)


class Refs:
    pass


class Attention:
    CHUNK = 512

    def __init__(self, r, kvg, h):
        self.r, self.h = r, h
        for j in range(NA):
            blk = r.blocks[0, j]
            leaf = lax.div(blk, 2)
            z, y, d = lax.div(leaf, 8), lax.rem(lax.div(leaf, 2), 4), lax.rem(leaf, 2)
            part = lax.rem(blk, 2)
            rows = pl.ds(j * BLK, BLK)
            r.ks[rows] = kvg[0, z, y, d, part]
            r.vs[rows] = kvg[1, y, z, d, part]
        cols = pl.ds(h * HEAD, HEAD)
        r.ks[pl.ds(ANC, TOK)] = r.bk[:, cols]
        r.vs[pl.ds(ANC, TOK)] = r.bv[:, cols]
        r.kt[...] = r.ks[...].T
        r.dk[...] = jnp.zeros((KEYS, HEAD), F32)
        r.dv[...] = jnp.zeros((KEYS, HEAD), F32)
        self.live = [j < r.count[0] for j in range(NA)]

    def columns(self, i):
        at = (self.h * GROUP + i) * HEAD
        return pl.ds(at if isinstance(i, int) else pl.multiple_of(at, HEAD), HEAD)

    def scores(self, ch, qh, top, total, e_ref):
        size = self.CHUNK
        n = size // BLK
        sc = contract_cols(self.r.ks[pl.ds(ch * size, size)], qh)
        high = None
        for j in range(n):
            part = sc[j * BLK : (j + 1) * BLK].reshape(8, 8, TOK).max(axis=0)
            part = jnp.where(self.live[ch * n + j], part, NEG)
            high = part if high is None else jnp.maximum(high, part)
        high = high.max(axis=0, keepdims=True) * EXP2_SCALE
        new = jnp.maximum(top, high)
        sums = None
        for j in range(n):
            slot = ch * n + j
            less = jnp.where(self.live[slot], new, 1e30)
            e = jnp.exp2(sc[j * BLK : (j + 1) * BLK] * EXP2_SCALE - less)
            e_ref[pl.ds(ch * size + j * BLK, BLK)] = e
            part = e.reshape(8, 8, TOK).sum(axis=0)
            sums = part if sums is None else sums + part
        return new, total * jnp.exp2(top - new) + sums

    def grads(self, ch, qh, gh, factor, delta, e, dqt):
        r = self.r
        size = e.shape[0]
        rows = pl.ds(ch * self.CHUNK, size)
        p = e * factor
        dp = contract_cols(r.vs[rows], gh)
        ds = (p * (dp - delta)).astype(BF)
        r.dv[rows] += jnp.dot(p.astype(BF), gh, preferred_element_type=F32)
        r.dk[rows] += jnp.dot(ds, qh, preferred_element_type=F32)
        term = jnp.dot(
            r.kt[:, ch * self.CHUNK : ch * self.CHUNK + size], ds, preferred_element_type=F32
        )
        return term if dqt is None else dqt + term

    def stage(self, i, e_ref, state, j, e_next):
        r = self.r
        dqt = None
        if j is not None:
            head = self.h * GROUP + j
            q_next = r.q[:, self.columns(j)]
            top, total = r.btop[head], r.bsum[head]
            tops = [top]
        if i is not None:
            cols = self.columns(i)
            qh, gh = r.q[:, cols], r.grad[:, cols]
            d = r.delta[self.h * GROUP + i]
        for ch in range(ANC // self.CHUNK):
            if j is not None:
                top, total = self.scores(ch, q_next, top, total, e_next)
                tops.append(top)
            if i is not None:
                e = e_ref[pl.ds(ch * self.CHUNK, self.CHUNK)]
                dqt = self.grads(ch, qh, gh, state[ch + 1 : ch + 2], d, e, dqt)
        if i is not None:
            dqt = self.grads(ANC // self.CHUNK, qh, gh, state[0:1], d, r.eb[self.h * GROUP + i], dqt)
            r.dq[:, cols] = (dqt * SCALE).T.astype(BF)
        if j is not None:
            inv = 1.0 / total.sum(axis=0, keepdims=True)
            return jnp.concatenate([jnp.exp2(t - top) * inv for t in tops], axis=0)


def head_start(r, h):
    ones = jnp.ones((8, HEAD), BF)
    keys = r.bk[:, h * HEAD : (h + 1) * HEAD]

    def one(i, carry):
        head = h * GROUP + i
        cols = pl.ds(pl.multiple_of(head * HEAD, HEAD), HEAD)
        prod = r.grad[:, cols].astype(F32) * r.out[:, cols].astype(F32)
        high = prod.astype(BF)
        low = (prod - high.astype(F32)).astype(BF)
        r.delta[head] = (contract_cols(ones, high) + contract_cols(ones, low))[0:1]
        sc = contract_cols(keys, r.q[:, cols])
        row = lax.broadcasted_iota(jnp.int32, (TOK, TOK), 0)
        sc = jnp.where(row <= lax.broadcasted_iota(jnp.int32, (TOK, TOK), 1), sc, NEG)
        top = sc.reshape(32, 8, TOK).max(axis=0).max(axis=0, keepdims=True) * EXP2_SCALE
        e = jnp.exp2(sc * EXP2_SCALE - top)
        r.eb[head] = e
        r.btop[head] = top
        r.bsum[head] = e.reshape(32, 8, TOK).sum(axis=0)
        return carry

    lax.fori_loop(0, GROUP, one, 0)


def tabulate(blocks, code):
    names = [blocks[0, j] for j in range(NA)]
    leaves = [lax.div(name, 2) for name in names]
    values = [4 * j + lax.rem(name, 2) + 1 for j, name in enumerate(names)]
    for o in range(32):
        terms = [jnp.where(leaf == o, value, 0) for leaf, value in zip(leaves, values, strict=True)]
        code[o] = functools.reduce(jnp.maximum, terms)


def tree_kernel(*refs):
    r = Refs()
    for name, ref in zip(NAMES, refs, strict=True):
        setattr(r, name, ref)
    me = Place()
    c = me.c
    kvg = [r.kvg0, r.kvg1, r.kvg2, r.kvg3]
    slots = [r.slots0, r.slots1, r.slots2, r.slots3]
    sib = [r.sib0, r.sib1, r.sib2, r.sib3]
    xt = [r.xt0, r.xt1, r.xt2, r.xt3]
    loads = [
        pltpu.make_async_copy(src, dst, r.lsem.at[n])
        for n, (src, dst) in enumerate(
            (
                (r.anc_hbm, r.anc),
                *[
                    (w_hbm.at[:, pl.ds(h * HEAD, HEAD)], w.at[:, pl.ds(h * HEAD, HEAD)])
                    for h in range(HEADS)
                    for w_hbm, w in ((r.wk_hbm, r.wk), (r.wv_hbm, r.wv))
                ],
                (r.q_hbm, r.q),
                (r.grad_hbm, r.grad),
                (r.out_hbm, r.out),
            )
        )
    ]
    for load in loads:
        load.start()
    greet(me)

    def sems(name, *at):
        return (
            lambda k: getattr(r, name + "ss").at[(*at, k)],
            lambda k: getattr(r, name + "sr").at[(*at, k)],
        )

    block_flow = Flow(me, *sems("b"))
    block_flow.go(0, lambda: r.blocks_hbm, lambda: r.sib_blocks_v, "sib")
    anc_flow = Flow(me, *sems("a"))
    for k, (to, owner) in enumerate((("x+", me.next), ("x-", me.last), ("x2", me.over))):
        cols = pl.ds(pl.multiple_of(owner * COLS, 128), COLS)
        anc_flow.go(k, lambda cols=cols: r.anc_hbm.at[:, cols], lambda: r.ancx.at[me.g, c], to)
    loads[0].wait()
    r.ancx[me.g, c] = r.anc[:, pl.ds(pl.multiple_of(me.g * COLS, 128), COLS)]
    gathers = [
        Gather(me, kvg[h], lambda t, h=h: r.own.at[t, h], *sems("g", h)) for h in range(HEADS)
    ]
    scatters = [
        LongScatter(me, h, r.dense, r.first, r.full, r.edge, r.edge_in, *sems("r", h))
        for h in range(HEADS)
    ]
    weights = [
        ShortScatter(me, h, r.part, None, r.wfull, r.wedge, r.wedge_in, *sems("w", h))
        for h in range(HEADS)
    ]
    overs = [Flow(me, *sems("o", h)) for h in range(HEADS)]
    pairs = [Flow(me, *sems("p", h)) for h in range(HEADS)]
    acrosses = [Flow(me, *sems("x", h)) for h in range(HEADS)]
    finals = [Flow(me, *sems("f", h)) for h in range(HEADS)]

    def anc_on():
        here = lambda: r.ancx.at[me.g, c]
        anc_flow.go(3, here, here, "sib")
        for k, owner in ((0, me.last), (1, me.next), (2, me.over)):
            anc_flow.got(k)
            there = lambda owner=owner: r.ancx.at[owner, c]
            anc_flow.go(4 + k, there, there, "sib")

    def anc_turn():
        anc_flow.got(3, 4, 5, 6)
        r.anct[...] = r.ancx[...].reshape(1024, COLS).T

    def slots_out(h):
        rows = pl.ds(0, ANC)
        slots[h][0] = (r.dk[rows] * SCALE).astype(BF).reshape(NA, BLK, HEAD)
        slots[h][1] = r.dv[rows].astype(BF).reshape(NA, BLK, HEAD)
        overs[h].go(0, lambda: slots[h].at[me.other], lambda: sib[h], "sib")
        rows = pl.ds(ANC, TOK)
        cols = pl.ds(h * HEAD, HEAD)
        r.dbk[:, cols] = (r.dk[rows] * SCALE).astype(BF)
        r.dbv[:, cols] = r.dv[rows].astype(BF)

    def build(h):
        overs[h].got(0)
        for i, row in enumerate((me.far, me.up, me.down, me.a)):
            for j in range(4):
                for d in range(2):
                    o = me.chip(row, j) * 2 + d
                    mine, theirs = r.code[o], r.sib_code[o]
                    x = slots[h][c, lax.div(mine, 4)]
                    y = sib[h][lax.div(theirs, 4)]
                    for block in range(2):
                        r.dense[h, row, j, d, pl.ds(block * BLK, BLK)] = add(
                            jnp.where(lax.rem(mine, 4) == block + 1, x, 0),
                            jnp.where(lax.rem(theirs, 4) == block + 1, y, 0),
                        )
            if i == 0:
                scatters[h].step(0)

    def totals(h):
        total = scatters[h].step(3).astype(BF)
        r.tot[h] = total
        xt[h][me.g] = total
        for k, to in enumerate(("x+", "x-", "x2")):
            acrosses[h].go(k, lambda: r.tot.at[h], lambda: xt[h].at[me.g], to)
        pairs[h].go(0, lambda: r.tot.at[h, me.other], lambda: r.pair.at[h], "sib")

    def weigh(h):
        acrosses[h].got(0, 1, 2)
        part = jnp.dot(
            r.anct[...], xt[h][...].reshape(1024, HEAD), preferred_element_type=F32
        ).astype(BF)
        blank = jnp.zeros((8, HEAD), BF)
        for n in range(16):
            x = jnp.concatenate([part[n * 56 : (n + 1) * 56], blank], axis=0)
            first, second = n // 4, n % 4
            row = first + c * (second - first)
            col = second + c * (first - second)
            r.part[h, row, col] = x.reshape(2, 32, HEAD)
        weights[h].step(0)

    def weighed(h):
        r.fin[h] = weights[h].step(2) * (1.0 / 128.0)
        finals[h].go(0, lambda: r.fin.at[h], lambda: r.fin_in.at[h], "sib")

    def state_grad():
        for h in range(HEADS):
            pairs[h].got(0)
        mine = jnp.concatenate([r.tot[h, c] for h in range(HEADS)], axis=1)
        other = jnp.concatenate([r.pair[h] for h in range(HEADS)], axis=1)
        keys = jnp.where(c == 0, mine, other)
        values = jnp.where(c == 0, other, mine)
        for n in range(0, WIDTH, 512):
            grad = contract_cols(keys, r.wk[pl.ds(n, 512)])
            grad = grad + contract_cols(values, r.wv[pl.ds(n, 512)])
            r.dstate[:, pl.ds(n, 512)] = grad.astype(BF)

    for h in range(HEADS):
        cols = pl.ds(h * HEAD, HEAD)
        for t, w in enumerate((r.wk, r.wv)):
            loads[1 + 2 * h + t].wait()
            kv = jnp.dot(r.anc[...], w[:, cols], preferred_element_type=F32)
            r.own[t, h] = kv.astype(BF).reshape(2, BLK, HEAD)
        gathers[h].step(0)
        if h:
            gathers[h - 1].step(1)
    gathers[3].step(1)
    for load in loads[9:]:
        load.wait()
    block_flow.got(0)
    names = pltpu.make_async_copy(r.sib_blocks_v, r.sib_blocks, r.lsem.at[12])
    names.start()
    tabulate(r.blocks, r.code)
    names.wait()
    tabulate(r.sib_blocks, r.sib_code)
    head_start(r, 0)
    gathers[0].step(2)
    gathers[1].step(2)
    head_start(r, 1)
    head_start(r, 2)
    gathers[0].step(3)
    gathers[2].step(2)
    head_start(r, 3)
    anc_on()
    gathers[0].step(4)
    gathers[1].step(3)
    gathers[3].step(2)
    anc_turn()

    def run(steps):
        for f, *args in steps:
            f(*args)

    def g(h, n):
        return (gathers[h].step, n)

    def s(h, n):
        return (scatters[h].step, n)

    def w(h, n):
        return (weights[h].step, n)

    plan = [[[] for _ in range(8)] for _ in range(HEADS)]
    for at, steps in {
        1: [g(1, 4)],
        2: [g(2, 3)],
        4: [g(2, 4)],
        5: [g(3, 3)],
        7: [g(3, 4)],
        10: [(build, 0)],
        14: [s(0, 1)],
        18: [(build, 1)],
        19: [s(0, 2)],
        22: [s(1, 1)],
        23: [(totals, 0)],
        26: [(build, 2)],
        27: [s(1, 2)],
        29: [(weigh, 0)],
        30: [s(2, 1)],
        31: [(totals, 1)],
    }.items():
        plan[at // 8][at % 8] = steps
    copies = []
    for h in range(HEADS):
        run(plan[h][0])
        gathers[h].step(5)
        att = Attention(r, kvg[h], h)
        state = att.stage(None, None, None, 0, r.e0)

        def two(i, state):
            for n in range(3):
                pl.when(i == n)(lambda n=n: run(plan[h][1 + 2 * n]))
            state = att.stage(2 * i, r.e0, state, 2 * i + 1, r.e1)
            for n in range(3):
                pl.when(i == n)(lambda n=n: run(plan[h][2 + 2 * n]))
            return att.stage(2 * i + 1, r.e1, state, 2 * i + 2, r.e0)

        if UNROLL:
            for i in range(3):
                run(plan[h][1 + 2 * i])
                state = att.stage(2 * i, r.e0, state, 2 * i + 1, r.e1)
                run(plan[h][2 + 2 * i])
                state = att.stage(2 * i + 1, r.e1, state, 2 * i + 2, r.e0)
        else:
            state = lax.fori_loop(0, 3, two, state)
        run(plan[h][7])
        att.stage(GROUP - 1, r.e0, state, None, None)
        slots_out(h)
        cols = pl.ds(h * GROUP * HEAD, GROUP * HEAD)
        copy = pltpu.make_async_copy(r.dq.at[:, cols], r.dq_hbm.at[:, cols], r.osem.at[h])
        copy.start()
        copies.append(copy)
    run([(build, 3), w(0, 1), s(2, 2), (weigh, 1), s(3, 1)])
    run([(weighed, 0), (totals, 2), w(1, 1), s(3, 2), (weighed, 1), (weigh, 2), (totals, 3)])
    run([w(2, 1), (state_grad,), (weighed, 2), (weigh, 3)])
    copy = pltpu.make_async_copy(r.dstate, r.dstate_hbm, r.osem.at[HEADS])
    copy.start()
    copies.append(copy)
    run([w(3, 1), (weighed, 3)])

    def rows_of(both):
        both = both.reshape(64, HEAD)
        return jnp.where(c == 0, both[0:28], both[28:56])

    for h in range(HEADS):
        finals[h].got(0)
        own, other = rows_of(r.fin[h]), rows_of(r.fin_in[h])
        cols = pl.ds(h * HEAD, HEAD)
        r.gk[:, cols] = jnp.where(c == 0, own, other)
        r.gv[:, cols] = jnp.where(c == 0, other, own)
    for flows in (gathers, scatters, weights, overs, pairs, acrosses, finals, [anc_flow, block_flow]):
        for flow in flows:
            flow.finish()
    for copy in copies:
        copy.wait()


UNROLL = True


def tree_call(blocks, count, anc, wk, wv, q, out, grad, bk, bv):
    hbm = pl.BlockSpec(memory_space=pl.ANY)
    smem = pl.BlockSpec(memory_space=pltpu.SMEM)
    vmem = pl.BlockSpec(memory_space=pltpu.VMEM)
    dma = pltpu.SemaphoreType.DMA

    def bf(*shape):
        return pltpu.VMEM(shape, BF)

    width = HEADS * HEAD
    scratch = [
        bf(OWN, WIDTH), bf(WIDTH, width), bf(WIDTH, width),
        bf(TOK, WIDTH), bf(TOK, WIDTH), bf(TOK, WIDTH),
        bf(2, HEADS, 2, BLK, HEAD),
        *[bf(2, 4, 4, 2, 2, BLK, HEAD)] * HEADS,
        bf(4, 2, OWN, COLS), bf(COLS, 1024),
        bf(KEYS, HEAD), bf(KEYS, HEAD), bf(HEAD, KEYS),
        pltpu.VMEM((HEADS * GROUP, TOK, TOK), F32), pltpu.VMEM((HEADS * GROUP, 1, TOK), F32),
        pltpu.VMEM((HEADS * GROUP, 8, TOK), F32), pltpu.VMEM((HEADS * GROUP, 1, TOK), F32),
        pltpu.VMEM((ANC, TOK), F32), pltpu.VMEM((ANC, TOK), F32),
        pltpu.VMEM((KEYS, HEAD), F32), pltpu.VMEM((KEYS, HEAD), F32),
        bf(TOK, WIDTH),
        *[bf(2, NA, BLK, HEAD)] * HEADS,
        *[bf(NA, BLK, HEAD)] * HEADS,
        bf(HEADS, 4, 4, 2, OWN, HEAD), bf(HEADS, 2, 2, 2, OWN, HEAD), bf(HEADS, 2, 4, 2, OWN, HEAD),
        bf(HEADS, 4, 2, OWN, HEAD), bf(HEADS, 3, 2, OWN, HEAD),
        bf(HEADS, 2, OWN, HEAD), bf(HEADS, OWN, HEAD),
        *[bf(4, 2, OWN, HEAD)] * HEADS,
        bf(HEADS, 4, 4, 2, 32, HEAD), bf(HEADS, 3, 4, 2, 32, HEAD),
        bf(HEADS, 4, 2, 32, HEAD), bf(HEADS, 3, 2, 32, HEAD),
        pltpu.VMEM((HEADS, 2, 32, HEAD), F32), pltpu.VMEM((HEADS, 2, 32, HEAD), F32),
        bf(OWN, WIDTH),
        pltpu.SMEM((32,), jnp.int32), pltpu.SMEM((32,), jnp.int32),
        pltpu.VMEM((1, NA), jnp.int32), pltpu.SMEM((1, NA), jnp.int32),
        dma((1,)), dma((1,)),
        dma((13,)), dma((HEADS + 1,)),
        dma((HEADS, 13)), dma((HEADS, 13)),
        dma((7,)), dma((7,)),
        dma((HEADS, 8)), dma((HEADS, 8)),
        dma((HEADS, 1)), dma((HEADS, 1)),
        dma((HEADS, 1)), dma((HEADS, 1)),
        dma((HEADS, 4)), dma((HEADS, 4)),
        dma((HEADS, 8)), dma((HEADS, 8)),
        dma((HEADS, 1)), dma((HEADS, 1)),
    ]
    return pl.pallas_call(
        tree_kernel,
        out_shape=(
            jax.ShapeDtypeStruct((TOK, WIDTH), BF),
            jax.ShapeDtypeStruct((TOK, width), BF),
            jax.ShapeDtypeStruct((TOK, width), BF),
            jax.ShapeDtypeStruct((OWN, WIDTH), BF),
            jax.ShapeDtypeStruct((28, width), F32),
            jax.ShapeDtypeStruct((28, width), F32),
        ),
        in_specs=[smem, hbm, smem] + [hbm] * 6 + [vmem] * 2,
        out_specs=(hbm, vmem, vmem, hbm, vmem, vmem),
        scratch_shapes=scratch,
        compiler_params=pltpu.CompilerParams(
            collective_id=0, has_side_effects=True, vmem_limit_bytes=60 * MIB
        ),
        name="tree",
    )(blocks, blocks, count, anc, wk, wv, q, out, grad, bk, bv)


def settle_kernel(*refs):
    n = (len(refs) - 2) // 3
    sem_in, sem_out = refs[-2:]
    views = []
    for k in range(n):
        src, dst, held = refs[k], refs[n + k], refs[2 * n + k]
        if k == 0:
            for part in range(4):
                rows = pl.ds(part * (TOK // 4), TOK // 4)
                views.append((src.at[rows], held.at[rows], dst.at[rows]))
        else:
            views.append((src, held, dst))
    ins = [pltpu.make_async_copy(x, y, sem_in.at[k]) for k, (x, y, _) in enumerate(views)]
    outs = [pltpu.make_async_copy(y, z, sem_out.at[k]) for k, (_, y, z) in enumerate(views)]
    for copy in ins:
        copy.start()
    for copy, out in zip(ins, outs, strict=True):
        copy.wait()
        out.start()
    for copy in outs:
        copy.wait()


def settle(arrays):
    hbm = pl.BlockSpec(memory_space=pl.ANY)
    count = len(arrays) + 3
    return pl.pallas_call(
        settle_kernel,
        out_shape=tuple(jax.ShapeDtypeStruct(x.shape, x.dtype) for x in arrays),
        in_specs=[hbm] * len(arrays),
        out_specs=(hbm,) * len(arrays),
        scratch_shapes=[pltpu.VMEM(x.shape, x.dtype) for x in arrays]
        + [pltpu.SemaphoreType.DMA((count,)), pltpu.SemaphoreType.DMA((count,))],
        compiler_params=pltpu.CompilerParams(vmem_limit_bytes=62 * MIB),
        name="settle",
    )(*arrays)


def on_device(q, bk, bv, out, grad, anc, wk, wv, blocks, count):
    return settle(tree_call(blocks, count, anc, wk, wv, q, out, grad, bk, bv))


def solution(mesh):
    rows = P(("dp", "leaf"), None)
    return jax.shard_map(
        on_device,
        mesh=mesh,
        in_specs=(rows, rows, rows, rows, rows, rows, P(), P(), rows, P(("dp", "leaf"))),
        out_specs=(rows,) * 6,
        check_vma=False,
    )
```

```python
import math

import jax
import jax.numpy as jnp
from jax import lax
from jax.experimental import pallas as pl
from jax.experimental.pallas import tpu as pltpu
from jax.sharding import PartitionSpec as P

BF = jnp.bfloat16
F32 = jnp.float32
WIDTH = 3584
HEADS = 4
GROUP = 7
HEAD = 128
NA = 16
BLK = 64
TOK = 256
ANC = NA * BLK
KEYS = ANC + TOK
OWN = 128
COLS = WIDTH // 4
SCALE = 1.0 / math.sqrt(HEAD)
EXP2_SCALE = SCALE * math.log2(math.e)
NEG = -1e30
MIB = 1024 * 1024


def contract_rows(left, right):
    return lax.dot_general(left, right, (((0,), (0,)), ((), ())), preferred_element_type=F32)


def contract_cols(left, right):
    return lax.dot_general(left, right, (((1,), (1,)), ((), ())), preferred_element_type=F32)


def wrap(v):
    return lax.rem(v + 4, 4)


class Place:
    def __init__(self):
        leaf = lax.axis_index("leaf")
        self.g = lax.axis_index("dp")
        self.leaf = leaf
        self.c = lax.rem(leaf, 2)
        self.other = 1 - self.c
        y = lax.rem(lax.div(leaf, 2), 4)
        z = lax.div(leaf, 8)
        self.a = z + self.c * (y - z)
        self.b = y + self.c * (z - y)
        self.up, self.down, self.far = (wrap(self.a + d) for d in (1, -1, 2))
        self.right, self.left, self.off = (wrap(self.b + d) for d in (1, -1, 2))
        self.next, self.last, self.over = (wrap(self.g + d) for d in (1, -1, 2))
        self.ring = {
            "b+": self.at(self.a, self.right),
            "b-": self.at(self.a, self.left),
            "a+": self.at(self.up, self.b),
            "a-": self.at(self.down, self.b),
            "a2": self.at(self.far, self.b),
            "b2": self.at(self.a, self.off),
            "x+": (self.next, leaf),
            "x-": (self.last, leaf),
            "x2": (self.over, leaf),
            "sib": (self.g, leaf + 1 - 2 * self.c),
        }

    def chip(self, a, b):
        return a * 4 + b + self.c * (3 * b - 3 * a)

    def at(self, a, b):
        return (self.g, self.chip(a, b) * 2 + self.c)


class Copy:
    def __init__(self, src, dst, ssem, rsem, to):
        self.parts = (src, dst, ssem, rsem, to)

    def make(self):
        src, dst, ssem, rsem, to = self.parts
        return pltpu.make_async_remote_copy(
            src_ref=src(),
            dst_ref=dst(),
            send_sem=ssem(),
            recv_sem=rsem(),
            device_id=to,
            device_id_type=pl.DeviceIdType.MESH,
        )

    def start(self):
        self.make().start()

    def arrive(self):
        self.make().wait_recv()

    def leave(self):
        self.make().wait_send()


def greet(me):
    barrier = pltpu.get_barrier_semaphore()
    for other in me.ring.values():
        pl.semaphore_signal(barrier, inc=1, device_id=other, device_id_type=pl.DeviceIdType.MESH)
    pl.semaphore_wait(barrier, len(me.ring))


class Flow:
    def __init__(self, me, ssem, rsem):
        self.me, self.ssem, self.rsem = me, ssem, rsem
        self.copies = {}

    def go(self, k, src, dst, to):
        copy = Copy(src, dst, lambda: self.ssem(k), lambda: self.rsem(k), self.me.ring[to])
        self.copies[k] = copy
        copy.start()

    def got(self, *ks):
        for k in ks:
            self.copies[k].arrive()

    def finish(self):
        for copy in self.copies.values():
            copy.leave()


class Gather(Flow):
    def __init__(self, me, kvg, own, ssem, rsem):
        super().__init__(me, ssem, rsem)
        self.kvg, self.own = kvg, own

    def step(self, n):
        me, kvg = self.me, self.kvg
        c, a, b = me.c, me.a, me.b
        if n == 0:
            self.go(0, lambda: self.own(me.other), lambda: kvg.at[me.other, b, a, c], "sib")
            kvg[c, a, b, c] = self.own(c)[...]
        elif n == 1:
            self.got(0)
            here = lambda: kvg.at[c, a, b]
            self.go(1, here, here, "b+")
            self.go(2, here, here, "b-")
            self.go(3, here, here, "b2")
        elif n == 2:
            self.got(1, 2, 3)
            row = lambda: kvg.at[c, a]
            self.go(5, row, row, "a+")
            self.go(6, row, row, "a-")
            self.go(9, row, row, "sib")
        elif n == 3:
            self.got(5)
            half = lambda: kvg.at[c, me.down, pl.ds(0, 2)]
            self.go(7, half, half, "a+")
            below = lambda: kvg.at[c, me.down]
            self.go(10, below, below, "sib")
            self.got(6)
            rest = lambda: kvg.at[c, me.up, pl.ds(2, 2)]
            self.go(8, rest, rest, "a-")
            above = lambda: kvg.at[c, me.up]
            self.go(11, above, above, "sib")
        elif n == 4:
            self.got(7, 8)
            far = lambda: kvg.at[c, me.far]
            self.go(12, far, far, "sib")
        else:
            self.got(9, 10, 11, 12)


def add(x, y):
    return (x.astype(F32) + y.astype(F32)).astype(BF)


class Scatter(Flow):
    def __init__(self, me, h, data, first, full, edge, edge_in, ssem, rsem):
        super().__init__(me, ssem, rsem)
        self.h = h
        self.data, self.first, self.full, self.edge, self.edge_in = data, first, full, edge, edge_in

    def spread(self, k):
        edge, edge_in, h, me = self.edge, self.edge_in, self.h, self.me
        for n, (to, b) in enumerate((("b+", me.right), ("b-", me.left), ("b2", me.off))):
            self.go(k + n, lambda b=b: edge.at[h, b], lambda n=n: edge_in.at[h, n], to)

    def total(self, k):
        self.got(k, k + 1, k + 2)
        total = self.edge[self.h, self.me.b].astype(F32)
        for n in range(3):
            total = total + self.edge_in[self.h, n].astype(F32)
        return total


class LongScatter(Scatter):
    def step(self, n):
        me, h = self.me, self.h
        data, first, full, edge = self.data, self.first, self.full, self.edge
        if n == 0:
            self.go(0, lambda: data.at[h, me.far, pl.ds(0, 2)], lambda: first.at[h, 0], "a+")
            self.go(1, lambda: data.at[h, me.far, pl.ds(2, 2)], lambda: first.at[h, 1], "a-")
        elif n == 1:
            self.got(0)
            low = pl.ds(0, 2)
            data[h, me.up, low] = add(data[h, me.up, low], first[h, 0])
            self.go(2, lambda: data.at[h, me.up], lambda: full.at[h, 0], "a+")
            self.got(1)
            high = pl.ds(2, 2)
            data[h, me.down, high] = add(data[h, me.down, high], first[h, 1])
            self.go(3, lambda: data.at[h, me.down], lambda: full.at[h, 1], "a-")
        elif n == 2:
            self.got(2, 3)
            for b in range(4):
                total = data[h, me.a, b].astype(F32) + full[h, 0, b].astype(F32)
                edge[h, b] = (total + full[h, 1, b].astype(F32)).astype(BF)
            self.spread(4)
        else:
            return self.total(4)


class ShortScatter(Scatter):
    def step(self, n):
        me, h = self.me, self.h
        data, full, edge = self.data, self.full, self.edge
        if n == 0:
            for k, (to, a) in enumerate((("a+", me.up), ("a-", me.down), ("a2", me.far))):
                self.go(k, lambda a=a: data.at[h, a], lambda k=k: full.at[h, k], to)
        elif n == 1:
            self.got(0, 1, 2)
            for b in range(4):
                total = data[h, me.a, b].astype(F32)
                for k in range(3):
                    total = total + full[h, k, b].astype(F32)
                edge[h, b] = total.astype(BF)
            self.spread(3)
        else:
            return self.total(3)


NAMES = (
    "blocks", "blocks_hbm", "count", "anc_hbm", "wk_hbm", "wv_hbm", "q_hbm", "out_hbm",
    "grad_hbm", "bk", "bv", "dq_hbm", "dbk", "dbv", "dstate_hbm", "gk", "gv", "anc", "wk", "wv",
    "q", "out", "grad", "own", "kvg0", "kvg1", "kvg2", "kvg3", "ancx", "anct", "ks", "vs", "kt",
    "eb", "btop", "bsum", "delta", "e0", "e1", "dk", "dv", "dq", "slots0", "slots1", "slots2",
    "slots3", "sib0", "sib1", "sib2", "sib3", "dense", "first", "full", "edge", "edge_in", "tot",
    "pair", "xt0", "xt1", "xt2", "xt3", "part", "wfull", "wedge", "wedge_in", "fin", "fin_in",
    "dstate", "code", "sib_code", "sib_blocks_v", "sib_blocks", "bss", "bsr", "lsem", "osem", "gss", "gsr", "ass", "asr", "rss", "rsr", "oss", "osr", "pss", "psr",
    "xss", "xsr", "wss", "wsr", "fss", "fsr",
)


class Refs:
    pass


class Attention:
    CHUNK = 512

    def __init__(self, r, kvg, h):
        self.r, self.h = r, h
        for j in range(NA):
            blk = r.blocks[0, j]
            leaf = lax.div(blk, 2)
            z, y, d = lax.div(leaf, 8), lax.rem(lax.div(leaf, 2), 4), lax.rem(leaf, 2)
            part = lax.rem(blk, 2)
            rows = pl.ds(j * BLK, BLK)
            r.ks[rows] = kvg[0, z, y, d, part]
            r.vs[rows] = kvg[1, y, z, d, part]
        cols = pl.ds(h * HEAD, HEAD)
        r.ks[pl.ds(ANC, TOK)] = r.bk[:, cols]
        r.vs[pl.ds(ANC, TOK)] = r.bv[:, cols]
        r.kt[...] = r.ks[...].T
        r.dk[...] = jnp.zeros((KEYS, HEAD), F32)
        r.dv[...] = jnp.zeros((KEYS, HEAD), F32)
        self.live = [j < r.count[0] for j in range(NA)]

    def columns(self, i):
        at = (self.h * GROUP + i) * HEAD
        return pl.ds(at if isinstance(i, int) else pl.multiple_of(at, HEAD), HEAD)

    def scores(self, ch, qh, top, total, e_ref):
        size = self.CHUNK
        n = size // BLK
        sc = contract_cols(self.r.ks[pl.ds(ch * size, size)], qh)
        high = None
        for j in range(n):
            part = sc[j * BLK : (j + 1) * BLK].reshape(8, 8, TOK).max(axis=0)
            part = jnp.where(self.live[ch * n + j], part, NEG)
            high = part if high is None else jnp.maximum(high, part)
        high = high.max(axis=0, keepdims=True) * EXP2_SCALE
        new = jnp.maximum(top, high)
        sums = None
        for j in range(n):
            slot = ch * n + j
            less = jnp.where(self.live[slot], new, 1e30)
            e = jnp.exp2(sc[j * BLK : (j + 1) * BLK] * EXP2_SCALE - less)
            e_ref[pl.ds(ch * size + j * BLK, BLK)] = e
            part = e.reshape(8, 8, TOK).sum(axis=0)
            sums = part if sums is None else sums + part
        return new, total * jnp.exp2(top - new) + sums

    def grads(self, ch, qh, gh, factor, delta, e, dqt):
        r = self.r
        size = e.shape[0]
        rows = pl.ds(ch * self.CHUNK, size)
        p = e * factor
        dp = contract_cols(r.vs[rows], gh)
        ds = (p * (dp - delta)).astype(BF)
        r.dv[rows] += jnp.dot(p.astype(BF), gh, preferred_element_type=F32)
        r.dk[rows] += jnp.dot(ds, qh, preferred_element_type=F32)
        term = jnp.dot(
            r.kt[:, ch * self.CHUNK : ch * self.CHUNK + size], ds, preferred_element_type=F32
        )
        return term if dqt is None else dqt + term

    def stage(self, i, e_ref, state, j, e_next):
        r = self.r
        dqt = None
        if j is not None:
            head = self.h * GROUP + j
            q_next = r.q[:, self.columns(j)]
            top, total = r.btop[head], r.bsum[head]
            tops = [top]
        if i is not None:
            cols = self.columns(i)
            qh, gh = r.q[:, cols], r.grad[:, cols]
            d = r.delta[self.h * GROUP + i]
        for ch in range(ANC // self.CHUNK):
            if j is not None:
                top, total = self.scores(ch, q_next, top, total, e_next)
                tops.append(top)
            if i is not None:
                e = e_ref[pl.ds(ch * self.CHUNK, self.CHUNK)]
                dqt = self.grads(ch, qh, gh, state[ch + 1 : ch + 2], d, e, dqt)
        if i is not None:
            dqt = self.grads(ANC // self.CHUNK, qh, gh, state[0:1], d, r.eb[self.h * GROUP + i], dqt)
            r.dq[:, cols] = (dqt * SCALE).T.astype(BF)
        if j is not None:
            inv = 1.0 / total.sum(axis=0, keepdims=True)
            return jnp.concatenate([jnp.exp2(t - top) * inv for t in tops], axis=0)


def head_start(r, h):
    ones = jnp.ones((8, HEAD), BF)
    keys = r.bk[:, h * HEAD : (h + 1) * HEAD]

    def one(i, carry):
        head = h * GROUP + i
        cols = pl.ds(pl.multiple_of(head * HEAD, HEAD), HEAD)
        prod = r.grad[:, cols].astype(F32) * r.out[:, cols].astype(F32)
        high = prod.astype(BF)
        low = (prod - high.astype(F32)).astype(BF)
        r.delta[head] = (contract_cols(ones, high) + contract_cols(ones, low))[0:1]
        sc = contract_cols(keys, r.q[:, cols])
        row = lax.broadcasted_iota(jnp.int32, (TOK, TOK), 0)
        sc = jnp.where(row <= lax.broadcasted_iota(jnp.int32, (TOK, TOK), 1), sc, NEG)
        top = sc.reshape(32, 8, TOK).max(axis=0).max(axis=0, keepdims=True) * EXP2_SCALE
        e = jnp.exp2(sc * EXP2_SCALE - top)
        r.eb[head] = e
        r.btop[head] = top
        r.bsum[head] = e.reshape(32, 8, TOK).sum(axis=0)
        return carry

    lax.fori_loop(0, GROUP, one, 0)


def tabulate(blocks, code):
    names = [blocks[0, j] for j in range(NA)]
    leaves = [lax.div(name, 2) for name in names]
    values = [4 * j + lax.rem(name, 2) + 1 for j, name in enumerate(names)]
    for o in range(32):
        terms = [jnp.where(leaf == o, value, 0) for leaf, value in zip(leaves, values, strict=True)]
        code[o] = jnp.minimum(sum(terms[1:], terms[0]), 4 * NA - 1)


def tree_kernel(*refs):
    r = Refs()
    for name, ref in zip(NAMES, refs, strict=True):
        setattr(r, name, ref)
    me = Place()
    c = me.c
    kvg = [r.kvg0, r.kvg1, r.kvg2, r.kvg3]
    slots = [r.slots0, r.slots1, r.slots2, r.slots3]
    sib = [r.sib0, r.sib1, r.sib2, r.sib3]
    xt = [r.xt0, r.xt1, r.xt2, r.xt3]
    loads = [
        pltpu.make_async_copy(src, dst, r.lsem.at[n])
        for n, (src, dst) in enumerate(
            (
                (r.anc_hbm, r.anc),
                *[
                    (w_hbm.at[:, pl.ds(h * HEAD, HEAD)], w.at[:, pl.ds(h * HEAD, HEAD)])
                    for h in range(HEADS)
                    for w_hbm, w in ((r.wk_hbm, r.wk), (r.wv_hbm, r.wv))
                ],
                (r.q_hbm, r.q),
                (r.grad_hbm, r.grad),
                (r.out_hbm, r.out),
            )
        )
    ]
    for load in loads:
        load.start()
    greet(me)

    def sems(name, *at):
        return (
            lambda k: getattr(r, name + "ss").at[(*at, k)],
            lambda k: getattr(r, name + "sr").at[(*at, k)],
        )

    block_flow = Flow(me, *sems("b"))
    block_flow.go(0, lambda: r.blocks_hbm, lambda: r.sib_blocks_v, "sib")
    anc_flow = Flow(me, *sems("a"))
    for k, (to, owner) in enumerate((("x+", me.next), ("x-", me.last), ("x2", me.over))):
        cols = pl.ds(pl.multiple_of(owner * COLS, 128), COLS)
        anc_flow.go(k, lambda cols=cols: r.anc_hbm.at[:, cols], lambda: r.ancx.at[me.g, c], to)
    loads[0].wait()
    r.ancx[me.g, c] = r.anc[:, pl.ds(pl.multiple_of(me.g * COLS, 128), COLS)]
    gathers = [
        Gather(me, kvg[h], lambda t, h=h: r.own.at[t, h], *sems("g", h)) for h in range(HEADS)
    ]
    scatters = [
        LongScatter(me, h, r.dense, r.first, r.full, r.edge, r.edge_in, *sems("r", h))
        for h in range(HEADS)
    ]
    weights = [
        ShortScatter(me, h, r.part, None, r.wfull, r.wedge, r.wedge_in, *sems("w", h))
        for h in range(HEADS)
    ]
    overs = [Flow(me, *sems("o", h)) for h in range(HEADS)]
    pairs = [Flow(me, *sems("p", h)) for h in range(HEADS)]
    acrosses = [Flow(me, *sems("x", h)) for h in range(HEADS)]
    finals = [Flow(me, *sems("f", h)) for h in range(HEADS)]

    def anc_on():
        here = lambda: r.ancx.at[me.g, c]
        anc_flow.go(3, here, here, "sib")
        for k, owner in ((0, me.last), (1, me.next), (2, me.over)):
            anc_flow.got(k)
            there = lambda owner=owner: r.ancx.at[owner, c]
            anc_flow.go(4 + k, there, there, "sib")

    def anc_turn():
        anc_flow.got(3, 4, 5, 6)
        r.anct[...] = r.ancx[...].reshape(1024, COLS).T

    def slots_out(h):
        rows = pl.ds(0, ANC)
        slots[h][0] = (r.dk[rows] * SCALE).astype(BF).reshape(NA, BLK, HEAD)
        slots[h][1] = r.dv[rows].astype(BF).reshape(NA, BLK, HEAD)
        overs[h].go(0, lambda: slots[h].at[me.other], lambda: sib[h], "sib")
        rows = pl.ds(ANC, TOK)
        cols = pl.ds(h * HEAD, HEAD)
        r.dbk[:, cols] = (r.dk[rows] * SCALE).astype(BF)
        r.dbv[:, cols] = r.dv[rows].astype(BF)

    def build(h):
        overs[h].got(0)
        for i, row in enumerate((me.far, me.up, me.down, me.a)):
            for j in range(4):
                for d in range(2):
                    o = me.chip(row, j) * 2 + d
                    mine, theirs = r.code[o], r.sib_code[o]
                    x = slots[h][c, lax.div(mine, 4)]
                    y = sib[h][lax.div(theirs, 4)]
                    for block in range(2):
                        r.dense[h, row, j, d, pl.ds(block * BLK, BLK)] = add(
                            jnp.where(lax.rem(mine, 4) == block + 1, x, 0),
                            jnp.where(lax.rem(theirs, 4) == block + 1, y, 0),
                        )
            if i == 0:
                scatters[h].step(0)

    def totals(h):
        total = scatters[h].step(3).astype(BF)
        r.tot[h] = total
        xt[h][me.g] = total
        for k, to in enumerate(("x+", "x-", "x2")):
            acrosses[h].go(k, lambda: r.tot.at[h], lambda: xt[h].at[me.g], to)
        pairs[h].go(0, lambda: r.tot.at[h, me.other], lambda: r.pair.at[h], "sib")

    def weigh(h):
        acrosses[h].got(0, 1, 2)
        part = jnp.dot(
            r.anct[...], xt[h][...].reshape(1024, HEAD), preferred_element_type=F32
        ).astype(BF)
        blank = jnp.zeros((8, HEAD), BF)
        for n in range(16):
            x = jnp.concatenate([part[n * 56 : (n + 1) * 56], blank], axis=0)
            first, second = n // 4, n % 4
            row = first + c * (second - first)
            col = second + c * (first - second)
            r.part[h, row, col] = x.reshape(2, 32, HEAD)
        weights[h].step(0)

    def weighed(h):
        r.fin[h] = weights[h].step(2) * (1.0 / 128.0)
        finals[h].go(0, lambda: r.fin.at[h], lambda: r.fin_in.at[h], "sib")

    def state_grad():
        for h in range(HEADS):
            pairs[h].got(0)
        mine = jnp.concatenate([r.tot[h, c] for h in range(HEADS)], axis=1)
        other = jnp.concatenate([r.pair[h] for h in range(HEADS)], axis=1)
        keys = jnp.where(c == 0, mine, other)
        values = jnp.where(c == 0, other, mine)
        for n in range(0, WIDTH, 512):
            grad = contract_cols(keys, r.wk[pl.ds(n, 512)])
            grad = grad + contract_cols(values, r.wv[pl.ds(n, 512)])
            r.dstate[:, pl.ds(n, 512)] = grad.astype(BF)

    for h in range(HEADS):
        cols = pl.ds(h * HEAD, HEAD)
        for t, w in enumerate((r.wk, r.wv)):
            loads[1 + 2 * h + t].wait()
            kv = jnp.dot(r.anc[...], w[:, cols], preferred_element_type=F32)
            r.own[t, h] = kv.astype(BF).reshape(2, BLK, HEAD)
        gathers[h].step(0)
        if h:
            gathers[h - 1].step(1)
    gathers[3].step(1)
    for load in loads[9:]:
        load.wait()
    block_flow.got(0)
    names = pltpu.make_async_copy(r.sib_blocks_v, r.sib_blocks, r.lsem.at[12])
    names.start()
    head_start(r, 0)
    gathers[0].step(2)
    gathers[1].step(2)
    head_start(r, 1)
    head_start(r, 2)
    gathers[0].step(3)
    gathers[2].step(2)
    head_start(r, 3)
    anc_on()
    gathers[0].step(4)
    gathers[1].step(3)
    gathers[3].step(2)
    anc_turn()
    names.wait()

    def run(steps):
        for f, *args in steps:
            f(*args)

    def g(h, n):
        return (gathers[h].step, n)

    def s(h, n):
        return (scatters[h].step, n)

    def w(h, n):
        return (weights[h].step, n)

    plan = [[[] for _ in range(8)] for _ in range(HEADS)]
    for at, steps in {
        1: [g(1, 4)],
        2: [g(2, 3)],
        3: [(tabulate, r.blocks, r.code)],
        4: [g(2, 4)],
        6: [(tabulate, r.sib_blocks, r.sib_code)],
        5: [g(3, 3)],
        7: [g(3, 4)],
        10: [(build, 0)],
        14: [s(0, 1)],
        18: [(build, 1)],
        19: [s(0, 2)],
        22: [s(1, 1)],
        23: [(totals, 0)],
        26: [(build, 2)],
        27: [s(1, 2)],
        29: [(weigh, 0)],
        30: [s(2, 1)],
        31: [(totals, 1)],
    }.items():
        plan[at // 8][at % 8] = steps
    copies = []
    for h in range(HEADS):
        run(plan[h][0])
        gathers[h].step(5)
        att = Attention(r, kvg[h], h)
        state = att.stage(None, None, None, 0, r.e0)

        def two(i, state):
            for n in range(3):
                pl.when(i == n)(lambda n=n: run(plan[h][1 + 2 * n]))
            state = att.stage(2 * i, r.e0, state, 2 * i + 1, r.e1)
            for n in range(3):
                pl.when(i == n)(lambda n=n: run(plan[h][2 + 2 * n]))
            return att.stage(2 * i + 1, r.e1, state, 2 * i + 2, r.e0)

        if UNROLL:
            for i in range(3):
                run(plan[h][1 + 2 * i])
                state = att.stage(2 * i, r.e0, state, 2 * i + 1, r.e1)
                run(plan[h][2 + 2 * i])
                state = att.stage(2 * i + 1, r.e1, state, 2 * i + 2, r.e0)
        else:
            state = lax.fori_loop(0, 3, two, state)
        run(plan[h][7])
        att.stage(GROUP - 1, r.e0, state, None, None)
        slots_out(h)
        cols = pl.ds(h * GROUP * HEAD, GROUP * HEAD)
        copy = pltpu.make_async_copy(r.dq.at[:, cols], r.dq_hbm.at[:, cols], r.osem.at[h])
        copy.start()
        copies.append(copy)
    run([(build, 3), w(0, 1), s(2, 2), (weigh, 1), s(3, 1)])
    run([(weighed, 0), (totals, 2), w(1, 1), s(3, 2), (weighed, 1), (weigh, 2), (totals, 3)])
    run([w(2, 1), (state_grad,), (weighed, 2), (weigh, 3)])
    copy = pltpu.make_async_copy(r.dstate, r.dstate_hbm, r.osem.at[HEADS])
    copy.start()
    copies.append(copy)
    run([w(3, 1), (weighed, 3)])

    def rows_of(both):
        both = both.reshape(64, HEAD)
        return jnp.where(c == 0, both[0:28], both[28:56])

    for h in range(HEADS):
        finals[h].got(0)
        own, other = rows_of(r.fin[h]), rows_of(r.fin_in[h])
        cols = pl.ds(h * HEAD, HEAD)
        r.gk[:, cols] = jnp.where(c == 0, own, other)
        r.gv[:, cols] = jnp.where(c == 0, other, own)
    for flows in (gathers, scatters, weights, overs, pairs, acrosses, finals, [anc_flow, block_flow]):
        for flow in flows:
            flow.finish()
    for copy in copies:
        copy.wait()


UNROLL = True


def tree_call(blocks, count, anc, wk, wv, q, out, grad, bk, bv):
    hbm = pl.BlockSpec(memory_space=pl.ANY)
    smem = pl.BlockSpec(memory_space=pltpu.SMEM)
    vmem = pl.BlockSpec(memory_space=pltpu.VMEM)
    dma = pltpu.SemaphoreType.DMA

    def bf(*shape):
        return pltpu.VMEM(shape, BF)

    width = HEADS * HEAD
    scratch = [
        bf(OWN, WIDTH), bf(WIDTH, width), bf(WIDTH, width),
        bf(TOK, WIDTH), bf(TOK, WIDTH), bf(TOK, WIDTH),
        bf(2, HEADS, 2, BLK, HEAD),
        *[bf(2, 4, 4, 2, 2, BLK, HEAD)] * HEADS,
        bf(4, 2, OWN, COLS), bf(COLS, 1024),
        bf(KEYS, HEAD), bf(KEYS, HEAD), bf(HEAD, KEYS),
        pltpu.VMEM((HEADS * GROUP, TOK, TOK), F32), pltpu.VMEM((HEADS * GROUP, 1, TOK), F32),
        pltpu.VMEM((HEADS * GROUP, 8, TOK), F32), pltpu.VMEM((HEADS * GROUP, 1, TOK), F32),
        pltpu.VMEM((ANC, TOK), F32), pltpu.VMEM((ANC, TOK), F32),
        pltpu.VMEM((KEYS, HEAD), F32), pltpu.VMEM((KEYS, HEAD), F32),
        bf(TOK, WIDTH),
        *[bf(2, NA, BLK, HEAD)] * HEADS,
        *[bf(NA, BLK, HEAD)] * HEADS,
        bf(HEADS, 4, 4, 2, OWN, HEAD), bf(HEADS, 2, 2, 2, OWN, HEAD), bf(HEADS, 2, 4, 2, OWN, HEAD),
        bf(HEADS, 4, 2, OWN, HEAD), bf(HEADS, 3, 2, OWN, HEAD),
        bf(HEADS, 2, OWN, HEAD), bf(HEADS, OWN, HEAD),
        *[bf(4, 2, OWN, HEAD)] * HEADS,
        bf(HEADS, 4, 4, 2, 32, HEAD), bf(HEADS, 3, 4, 2, 32, HEAD),
        bf(HEADS, 4, 2, 32, HEAD), bf(HEADS, 3, 2, 32, HEAD),
        pltpu.VMEM((HEADS, 2, 32, HEAD), F32), pltpu.VMEM((HEADS, 2, 32, HEAD), F32),
        bf(OWN, WIDTH),
        pltpu.SMEM((32,), jnp.int32), pltpu.SMEM((32,), jnp.int32),
        pltpu.VMEM((1, NA), jnp.int32), pltpu.SMEM((1, NA), jnp.int32),
        dma((1,)), dma((1,)),
        dma((13,)), dma((HEADS + 1,)),
        dma((HEADS, 13)), dma((HEADS, 13)),
        dma((7,)), dma((7,)),
        dma((HEADS, 8)), dma((HEADS, 8)),
        dma((HEADS, 1)), dma((HEADS, 1)),
        dma((HEADS, 1)), dma((HEADS, 1)),
        dma((HEADS, 4)), dma((HEADS, 4)),
        dma((HEADS, 8)), dma((HEADS, 8)),
        dma((HEADS, 1)), dma((HEADS, 1)),
    ]
    return pl.pallas_call(
        tree_kernel,
        out_shape=(
            jax.ShapeDtypeStruct((TOK, WIDTH), BF),
            jax.ShapeDtypeStruct((TOK, width), BF),
            jax.ShapeDtypeStruct((TOK, width), BF),
            jax.ShapeDtypeStruct((OWN, WIDTH), BF),
            jax.ShapeDtypeStruct((28, width), F32),
            jax.ShapeDtypeStruct((28, width), F32),
        ),
        in_specs=[smem, hbm, smem] + [hbm] * 6 + [vmem] * 2,
        out_specs=(hbm, vmem, vmem, hbm, vmem, vmem),
        scratch_shapes=scratch,
        compiler_params=pltpu.CompilerParams(
            collective_id=0, has_side_effects=True, vmem_limit_bytes=60 * MIB
        ),
        name="tree",
    )(blocks, blocks, count, anc, wk, wv, q, out, grad, bk, bv)


def settle_kernel(*refs):
    n = (len(refs) - 2) // 3
    sem_in, sem_out = refs[-2:]
    views = []
    for k in range(n):
        src, dst, held = refs[k], refs[n + k], refs[2 * n + k]
        if k == 0:
            for part in range(4):
                rows = pl.ds(part * (TOK // 4), TOK // 4)
                views.append((src.at[rows], held.at[rows], dst.at[rows]))
        else:
            views.append((src, held, dst))
    ins = [pltpu.make_async_copy(x, y, sem_in.at[k]) for k, (x, y, _) in enumerate(views)]
    outs = [pltpu.make_async_copy(y, z, sem_out.at[k]) for k, (_, y, z) in enumerate(views)]
    for copy in ins:
        copy.start()
    for copy, out in zip(ins, outs, strict=True):
        copy.wait()
        out.start()
    for copy in outs:
        copy.wait()


def settle(arrays):
    hbm = pl.BlockSpec(memory_space=pl.ANY)
    count = len(arrays) + 3
    return pl.pallas_call(
        settle_kernel,
        out_shape=tuple(jax.ShapeDtypeStruct(x.shape, x.dtype) for x in arrays),
        in_specs=[hbm] * len(arrays),
        out_specs=(hbm,) * len(arrays),
        scratch_shapes=[pltpu.VMEM(x.shape, x.dtype) for x in arrays]
        + [pltpu.SemaphoreType.DMA((count,)), pltpu.SemaphoreType.DMA((count,))],
        compiler_params=pltpu.CompilerParams(vmem_limit_bytes=62 * MIB),
        name="settle",
    )(*arrays)


def on_device(q, bk, bv, out, grad, anc, wk, wv, blocks, count):
    return settle(tree_call(blocks, count, anc, wk, wv, q, out, grad, bk, bv))


def solution(mesh):
    rows = P(("dp", "leaf"), None)
    return jax.shard_map(
        on_device,
        mesh=mesh,
        in_specs=(rows, rows, rows, rows, rows, rows, P(), P(), rows, P(("dp", "leaf"))),
        out_specs=(rows,) * 6,
        check_vma=False,
    )
```

```python
import math

import jax
import jax.numpy as jnp
from jax import lax
from jax.experimental import pallas as pl
from jax.experimental.pallas import tpu as pltpu
from jax.sharding import PartitionSpec as P

BF = jnp.bfloat16
F32 = jnp.float32
WIDTH = 3584
HEADS = 4
GROUP = 7
HEAD = 128
NA = 16
SURE = 12
BLK = 64
TOK = 256
ANC = NA * BLK
KEYS = ANC + TOK
OWN = 128
COLS = WIDTH // 4
SCALE = 1.0 / math.sqrt(HEAD)
EXP2_SCALE = SCALE * math.log2(math.e)
NEG = -1e30
MIB = 1024 * 1024


def contract_rows(left, right):
    return lax.dot_general(left, right, (((0,), (0,)), ((), ())), preferred_element_type=F32)


def contract_cols(left, right):
    return lax.dot_general(left, right, (((1,), (1,)), ((), ())), preferred_element_type=F32)


def wrap(v):
    return lax.rem(v + 4, 4)


class Place:
    def __init__(self):
        leaf = lax.axis_index("leaf")
        self.g = lax.axis_index("dp")
        self.leaf = leaf
        self.c = lax.rem(leaf, 2)
        self.other = 1 - self.c
        y = lax.rem(lax.div(leaf, 2), 4)
        z = lax.div(leaf, 8)
        self.a = z + self.c * (y - z)
        self.b = y + self.c * (z - y)
        self.up, self.down, self.far = (wrap(self.a + d) for d in (1, -1, 2))
        self.right, self.left, self.off = (wrap(self.b + d) for d in (1, -1, 2))
        self.next, self.last, self.over = (wrap(self.g + d) for d in (1, -1, 2))
        self.ring = {
            "b+": self.at(self.a, self.right),
            "b-": self.at(self.a, self.left),
            "a+": self.at(self.up, self.b),
            "a-": self.at(self.down, self.b),
            "a2": self.at(self.far, self.b),
            "b2": self.at(self.a, self.off),
            "x+": (self.next, leaf),
            "x-": (self.last, leaf),
            "x2": (self.over, leaf),
            "sib": (self.g, leaf + 1 - 2 * self.c),
        }

    def chip(self, a, b):
        return a * 4 + b + self.c * (3 * b - 3 * a)

    def at(self, a, b):
        return (self.g, self.chip(a, b) * 2 + self.c)


class Copy:
    def __init__(self, src, dst, ssem, rsem, to):
        self.parts = (src, dst, ssem, rsem, to)

    def make(self):
        src, dst, ssem, rsem, to = self.parts
        return pltpu.make_async_remote_copy(
            src_ref=src(),
            dst_ref=dst(),
            send_sem=ssem(),
            recv_sem=rsem(),
            device_id=to,
            device_id_type=pl.DeviceIdType.MESH,
        )

    def start(self):
        self.make().start()

    def arrive(self):
        self.make().wait_recv()

    def leave(self):
        self.make().wait_send()


def greet(me):
    barrier = pltpu.get_barrier_semaphore()
    for other in me.ring.values():
        pl.semaphore_signal(barrier, inc=1, device_id=other, device_id_type=pl.DeviceIdType.MESH)
    pl.semaphore_wait(barrier, len(me.ring))


class Flow:
    def __init__(self, me, ssem, rsem):
        self.me, self.ssem, self.rsem = me, ssem, rsem
        self.copies = {}

    def go(self, k, src, dst, to):
        copy = Copy(src, dst, lambda: self.ssem(k), lambda: self.rsem(k), self.me.ring[to])
        self.copies[k] = copy
        copy.start()

    def got(self, *ks):
        for k in ks:
            self.copies[k].arrive()

    def finish(self):
        for copy in self.copies.values():
            copy.leave()


class Gather(Flow):
    def __init__(self, me, kvg, own, ssem, rsem):
        super().__init__(me, ssem, rsem)
        self.kvg, self.own = kvg, own

    def step(self, n):
        me, kvg = self.me, self.kvg
        c, a, b = me.c, me.a, me.b
        if n == 0:
            self.go(0, lambda: self.own(me.other), lambda: kvg.at[me.other, b, a, c], "sib")
            kvg[c, a, b, c] = self.own(c)[...]
        elif n == 1:
            self.got(0)
            here = lambda: kvg.at[c, a, b]
            self.go(1, here, here, "b+")
            self.go(2, here, here, "b-")
            self.go(3, here, here, "b2")
        elif n == 2:
            self.got(1, 2, 3)
            row = lambda: kvg.at[c, a]
            self.go(5, row, row, "a+")
            self.go(6, row, row, "a-")
            self.go(9, row, row, "sib")
        elif n == 3:
            self.got(5)
            half = lambda: kvg.at[c, me.down, pl.ds(0, 2)]
            self.go(7, half, half, "a+")
            below = lambda: kvg.at[c, me.down]
            self.go(10, below, below, "sib")
            self.got(6)
            rest = lambda: kvg.at[c, me.up, pl.ds(2, 2)]
            self.go(8, rest, rest, "a-")
            above = lambda: kvg.at[c, me.up]
            self.go(11, above, above, "sib")
        elif n == 4:
            self.got(7, 8)
            far = lambda: kvg.at[c, me.far]
            self.go(12, far, far, "sib")
        else:
            self.got(9, 10, 11, 12)


def add(x, y):
    return (x.astype(F32) + y.astype(F32)).astype(BF)


class Scatter(Flow):
    def __init__(self, me, h, data, first, full, edge, edge_in, ssem, rsem):
        super().__init__(me, ssem, rsem)
        self.h = h
        self.data, self.first, self.full, self.edge, self.edge_in = data, first, full, edge, edge_in

    def spread(self, k):
        edge, edge_in, h, me = self.edge, self.edge_in, self.h, self.me
        for n, (to, b) in enumerate((("b+", me.right), ("b-", me.left), ("b2", me.off))):
            self.go(k + n, lambda b=b: edge.at[h, b], lambda n=n: edge_in.at[h, n], to)

    def total(self, k):
        self.got(k, k + 1, k + 2)
        total = self.edge[self.h, self.me.b].astype(F32)
        for n in range(3):
            total = total + self.edge_in[self.h, n].astype(F32)
        return total


class LongScatter(Scatter):
    def step(self, n):
        me, h = self.me, self.h
        data, first, full, edge = self.data, self.first, self.full, self.edge
        if n == 0:
            self.go(0, lambda: data.at[h, me.far, pl.ds(0, 2)], lambda: first.at[h, 0], "a+")
            self.go(1, lambda: data.at[h, me.far, pl.ds(2, 2)], lambda: first.at[h, 1], "a-")
        elif n == 1:
            self.got(0)
            low = pl.ds(0, 2)
            data[h, me.up, low] = add(data[h, me.up, low], first[h, 0])
            self.go(2, lambda: data.at[h, me.up], lambda: full.at[h, 0], "a+")
            self.got(1)
            high = pl.ds(2, 2)
            data[h, me.down, high] = add(data[h, me.down, high], first[h, 1])
            self.go(3, lambda: data.at[h, me.down], lambda: full.at[h, 1], "a-")
        elif n == 2:
            self.got(2, 3)
            for b in range(4):
                total = data[h, me.a, b].astype(F32) + full[h, 0, b].astype(F32)
                edge[h, b] = (total + full[h, 1, b].astype(F32)).astype(BF)
            self.spread(4)
        else:
            return self.total(4)


class ShortScatter(Scatter):
    def step(self, n):
        me, h = self.me, self.h
        data, full, edge = self.data, self.full, self.edge
        if n == 0:
            for k, (to, a) in enumerate((("a+", me.up), ("a-", me.down), ("a2", me.far))):
                self.go(k, lambda a=a: data.at[h, a], lambda k=k: full.at[h, k], to)
        elif n == 1:
            self.got(0, 1, 2)
            for b in range(4):
                total = data[h, me.a, b].astype(F32)
                for k in range(3):
                    total = total + full[h, k, b].astype(F32)
                edge[h, b] = total.astype(BF)
            self.spread(3)
        else:
            return self.total(3)


NAMES = (
    "blocks", "blocks_hbm", "count", "anc_hbm", "wk_hbm", "wv_hbm", "q_hbm", "out_hbm",
    "grad_hbm", "bk", "bv", "dq_hbm", "dbk", "dbv", "dstate_hbm", "gk", "gv", "anc", "wk", "wv",
    "q", "out", "grad", "own", "kvg0", "kvg1", "kvg2", "kvg3", "ancx", "anct", "ks", "vs", "kt",
    "eb", "btop", "bsum", "delta", "e0", "e1", "dk", "dv", "dq", "slots0", "slots1", "slots2",
    "slots3", "sib0", "sib1", "sib2", "sib3", "dense", "first", "full", "edge", "edge_in", "tot",
    "pair", "xt0", "xt1", "xt2", "xt3", "part", "wfull", "wedge", "wedge_in", "fin", "fin_in",
    "dstate", "code", "sib_code", "sib_blocks_v", "sib_blocks", "bss", "bsr", "lsem", "osem", "gss", "gsr", "ass", "asr", "rss", "rsr", "oss", "osr", "pss", "psr",
    "xss", "xsr", "wss", "wsr", "fss", "fsr",
)


class Refs:
    pass


class Attention:
    CHUNK = 1024

    def __init__(self, r, kvg, h):
        self.r, self.h = r, h
        for j in range(NA):
            blk = r.blocks[0, j]
            leaf = lax.div(blk, 2)
            z, y, d = lax.div(leaf, 8), lax.rem(lax.div(leaf, 2), 4), lax.rem(leaf, 2)
            part = lax.rem(blk, 2)
            rows = pl.ds(j * BLK, BLK)
            r.ks[rows] = kvg[0, z, y, d, part]
            r.vs[rows] = kvg[1, y, z, d, part]
        cols = pl.ds(h * HEAD, HEAD)
        r.ks[pl.ds(ANC, TOK)] = r.bk[:, cols]
        r.vs[pl.ds(ANC, TOK)] = r.bv[:, cols]
        r.kt[...] = r.ks[...].T
        r.dk[...] = jnp.zeros((KEYS, HEAD), F32)
        r.dv[...] = jnp.zeros((KEYS, HEAD), F32)
        self.live = [j < r.count[0] for j in range(NA)]

    def columns(self, i):
        at = (self.h * GROUP + i) * HEAD
        return pl.ds(at if isinstance(i, int) else pl.multiple_of(at, HEAD), HEAD)

    def scores(self, ch, qh, top, total, e_ref):
        size = self.CHUNK
        n = size // BLK
        sc = contract_cols(self.r.ks[pl.ds(ch * size, size)], qh)
        high = None
        for j in range(n):
            part = sc[j * BLK : (j + 1) * BLK].reshape(8, 8, TOK).max(axis=0)
            if ch * n + j >= SURE:
                part = jnp.where(self.live[ch * n + j], part, NEG)
            high = part if high is None else jnp.maximum(high, part)
        high = high.max(axis=0, keepdims=True) * EXP2_SCALE
        new = jnp.maximum(top, high)
        sums = None
        for j in range(n):
            slot = ch * n + j
            less = new if slot < SURE else jnp.where(self.live[slot], new, 1e30)
            e = jnp.exp2(sc[j * BLK : (j + 1) * BLK] * EXP2_SCALE - less)
            e_ref[pl.ds(ch * size + j * BLK, BLK)] = e
            part = e.reshape(8, 8, TOK).sum(axis=0)
            sums = part if sums is None else sums + part
        return new, total * jnp.exp2(top - new) + sums

    def grads(self, ch, qh, gh, factor, delta, e, dqt):
        r = self.r
        size = e.shape[0]
        rows = pl.ds(ch * self.CHUNK, size)
        p = e * factor
        dp = contract_cols(r.vs[rows], gh)
        ds = (p * (dp - delta)).astype(BF)
        r.dv[rows] += jnp.dot(p.astype(BF), gh, preferred_element_type=F32)
        r.dk[rows] += jnp.dot(ds, qh, preferred_element_type=F32)
        term = jnp.dot(
            r.kt[:, ch * self.CHUNK : ch * self.CHUNK + size], ds, preferred_element_type=F32
        )
        return term if dqt is None else dqt + term

    def stage(self, i, e_ref, state, j, e_next):
        r = self.r
        dqt = None
        if j is not None:
            head = self.h * GROUP + j
            q_next = r.q[:, self.columns(j)]
            top, total = r.btop[head], r.bsum[head]
            tops = [top]
        if i is not None:
            cols = self.columns(i)
            qh, gh = r.q[:, cols], r.grad[:, cols]
            d = r.delta[self.h * GROUP + i]
        for ch in range(ANC // self.CHUNK):
            if j is not None:
                top, total = self.scores(ch, q_next, top, total, e_next)
                tops.append(top)
            if i is not None:
                e = e_ref[pl.ds(ch * self.CHUNK, self.CHUNK)]
                dqt = self.grads(ch, qh, gh, state[ch + 1 : ch + 2], d, e, dqt)
        if i is not None:
            dqt = self.grads(ANC // self.CHUNK, qh, gh, state[0:1], d, r.eb[self.h * GROUP + i], dqt)
            r.dq[:, cols] = (dqt * SCALE).T.astype(BF)
        if j is not None:
            inv = 1.0 / total.sum(axis=0, keepdims=True)
            return jnp.concatenate([jnp.exp2(t - top) * inv for t in tops], axis=0)


def head_start(r, h):
    ones = jnp.ones((8, HEAD), BF)
    keys = r.bk[:, h * HEAD : (h + 1) * HEAD]

    def one(i, carry):
        head = h * GROUP + i
        cols = pl.ds(pl.multiple_of(head * HEAD, HEAD), HEAD)
        prod = r.grad[:, cols].astype(F32) * r.out[:, cols].astype(F32)
        high = prod.astype(BF)
        low = (prod - high.astype(F32)).astype(BF)
        r.delta[head] = (contract_cols(ones, high) + contract_cols(ones, low))[0:1]
        sc = contract_cols(keys, r.q[:, cols])
        row = lax.broadcasted_iota(jnp.int32, (TOK, TOK), 0)
        sc = jnp.where(row <= lax.broadcasted_iota(jnp.int32, (TOK, TOK), 1), sc, NEG)
        top = sc.reshape(32, 8, TOK).max(axis=0).max(axis=0, keepdims=True) * EXP2_SCALE
        e = jnp.exp2(sc * EXP2_SCALE - top)
        r.eb[head] = e
        r.btop[head] = top
        r.bsum[head] = e.reshape(32, 8, TOK).sum(axis=0)
        return carry

    lax.fori_loop(0, GROUP, one, 0)


def tabulate(blocks, code):
    names = [blocks[0, j] for j in range(NA)]
    leaves = [lax.div(name, 2) for name in names]
    values = [4 * j + lax.rem(name, 2) + 1 for j, name in enumerate(names)]
    for o in range(32):
        terms = [jnp.where(leaf == o, value, 0) for leaf, value in zip(leaves, values, strict=True)]
        code[o] = jnp.minimum(sum(terms[1:], terms[0]), 4 * NA - 1)


def tree_kernel(*refs):
    r = Refs()
    for name, ref in zip(NAMES, refs, strict=True):
        setattr(r, name, ref)
    me = Place()
    c = me.c
    kvg = [r.kvg0, r.kvg1, r.kvg2, r.kvg3]
    slots = [r.slots0, r.slots1, r.slots2, r.slots3]
    sib = [r.sib0, r.sib1, r.sib2, r.sib3]
    xt = [r.xt0, r.xt1, r.xt2, r.xt3]
    loads = [
        pltpu.make_async_copy(src, dst, r.lsem.at[n])
        for n, (src, dst) in enumerate(
            (
                (r.anc_hbm, r.anc),
                *[
                    (w_hbm.at[:, pl.ds(h * HEAD, HEAD)], w.at[:, pl.ds(h * HEAD, HEAD)])
                    for h in range(HEADS)
                    for w_hbm, w in ((r.wk_hbm, r.wk), (r.wv_hbm, r.wv))
                ],
                (r.q_hbm, r.q),
                (r.grad_hbm, r.grad),
                (r.out_hbm, r.out),
            )
        )
    ]
    for load in loads:
        load.start()
    greet(me)

    def sems(name, *at):
        return (
            lambda k: getattr(r, name + "ss").at[(*at, k)],
            lambda k: getattr(r, name + "sr").at[(*at, k)],
        )

    block_flow = Flow(me, *sems("b"))
    block_flow.go(0, lambda: r.blocks_hbm, lambda: r.sib_blocks_v, "sib")
    anc_flow = Flow(me, *sems("a"))
    for k, (to, owner) in enumerate((("x+", me.next), ("x-", me.last), ("x2", me.over))):
        cols = pl.ds(pl.multiple_of(owner * COLS, 128), COLS)
        anc_flow.go(k, lambda cols=cols: r.anc_hbm.at[:, cols], lambda: r.ancx.at[me.g, c], to)
    loads[0].wait()
    r.ancx[me.g, c] = r.anc[:, pl.ds(pl.multiple_of(me.g * COLS, 128), COLS)]
    gathers = [
        Gather(me, kvg[h], lambda t, h=h: r.own.at[t, h], *sems("g", h)) for h in range(HEADS)
    ]
    scatters = [
        LongScatter(me, h, r.dense, r.first, r.full, r.edge, r.edge_in, *sems("r", h))
        for h in range(HEADS)
    ]
    weights = [
        ShortScatter(me, h, r.part, None, r.wfull, r.wedge, r.wedge_in, *sems("w", h))
        for h in range(HEADS)
    ]
    overs = [Flow(me, *sems("o", h)) for h in range(HEADS)]
    pairs = [Flow(me, *sems("p", h)) for h in range(HEADS)]
    acrosses = [Flow(me, *sems("x", h)) for h in range(HEADS)]
    finals = [Flow(me, *sems("f", h)) for h in range(HEADS)]

    def anc_on():
        here = lambda: r.ancx.at[me.g, c]
        anc_flow.go(3, here, here, "sib")
        for k, owner in ((0, me.last), (1, me.next), (2, me.over)):
            anc_flow.got(k)
            there = lambda owner=owner: r.ancx.at[owner, c]
            anc_flow.go(4 + k, there, there, "sib")

    def anc_turn():
        anc_flow.got(3, 4, 5, 6)
        r.anct[...] = r.ancx[...].reshape(1024, COLS).T

    def slots_out(h):
        rows = pl.ds(0, ANC)
        slots[h][0] = (r.dk[rows] * SCALE).astype(BF).reshape(NA, BLK, HEAD)
        slots[h][1] = r.dv[rows].astype(BF).reshape(NA, BLK, HEAD)
        overs[h].go(0, lambda: slots[h].at[me.other], lambda: sib[h], "sib")
        rows = pl.ds(ANC, TOK)
        cols = pl.ds(h * HEAD, HEAD)
        r.dbk[:, cols] = (r.dk[rows] * SCALE).astype(BF)
        r.dbv[:, cols] = r.dv[rows].astype(BF)

    def build(h):
        overs[h].got(0)
        for i, row in enumerate((me.far, me.up, me.down, me.a)):
            for j in range(4):
                for d in range(2):
                    o = me.chip(row, j) * 2 + d
                    mine, theirs = r.code[o], r.sib_code[o]
                    x = slots[h][c, lax.div(mine, 4)]
                    y = sib[h][lax.div(theirs, 4)]
                    for block in range(2):
                        r.dense[h, row, j, d, pl.ds(block * BLK, BLK)] = add(
                            jnp.where(lax.rem(mine, 4) == block + 1, x, 0),
                            jnp.where(lax.rem(theirs, 4) == block + 1, y, 0),
                        )
            if i == 0:
                scatters[h].step(0)

    def totals(h):
        total = scatters[h].step(3).astype(BF)
        r.tot[h] = total
        xt[h][me.g] = total
        for k, to in enumerate(("x+", "x-", "x2")):
            acrosses[h].go(k, lambda: r.tot.at[h], lambda: xt[h].at[me.g], to)
        pairs[h].go(0, lambda: r.tot.at[h, me.other], lambda: r.pair.at[h], "sib")

    def weigh(h):
        acrosses[h].got(0, 1, 2)
        part = jnp.dot(
            r.anct[...], xt[h][...].reshape(1024, HEAD), preferred_element_type=F32
        ).astype(BF)
        blank = jnp.zeros((8, HEAD), BF)
        for n in range(16):
            x = jnp.concatenate([part[n * 56 : (n + 1) * 56], blank], axis=0)
            first, second = n // 4, n % 4
            row = first + c * (second - first)
            col = second + c * (first - second)
            r.part[h, row, col] = x.reshape(2, 32, HEAD)
        weights[h].step(0)

    def weighed(h):
        r.fin[h] = weights[h].step(2) * (1.0 / 128.0)
        finals[h].go(0, lambda: r.fin.at[h], lambda: r.fin_in.at[h], "sib")

    def state_grad():
        for h in range(HEADS):
            pairs[h].got(0)
        mine = jnp.concatenate([r.tot[h, c] for h in range(HEADS)], axis=1)
        other = jnp.concatenate([r.pair[h] for h in range(HEADS)], axis=1)
        keys = jnp.where(c == 0, mine, other)
        values = jnp.where(c == 0, other, mine)
        for n in range(0, WIDTH, 512):
            grad = contract_cols(keys, r.wk[pl.ds(n, 512)])
            grad = grad + contract_cols(values, r.wv[pl.ds(n, 512)])
            r.dstate[:, pl.ds(n, 512)] = grad.astype(BF)

    for h in range(HEADS):
        cols = pl.ds(h * HEAD, HEAD)
        for t, w in enumerate((r.wk, r.wv)):
            loads[1 + 2 * h + t].wait()
            kv = jnp.dot(r.anc[...], w[:, cols], preferred_element_type=F32)
            r.own[t, h] = kv.astype(BF).reshape(2, BLK, HEAD)
        gathers[h].step(0)
        if h:
            gathers[h - 1].step(1)
    gathers[3].step(1)
    for load in loads[9:]:
        load.wait()
    block_flow.got(0)
    names = pltpu.make_async_copy(r.sib_blocks_v, r.sib_blocks, r.lsem.at[12])
    names.start()
    head_start(r, 0)
    gathers[0].step(2)
    gathers[1].step(2)
    head_start(r, 1)
    head_start(r, 2)
    gathers[0].step(3)
    gathers[2].step(2)
    head_start(r, 3)
    gathers[0].step(4)
    gathers[1].step(3)
    gathers[3].step(2)
    anc_on()
    names.wait()

    def run(steps):
        for f, *args in steps:
            f(*args)

    def g(h, n):
        return (gathers[h].step, n)

    def s(h, n):
        return (scatters[h].step, n)

    def w(h, n):
        return (weights[h].step, n)

    plan = [[[] for _ in range(8)] for _ in range(HEADS)]
    for at, steps in {
        1: [g(2, 3)],
        3: [(tabulate, r.blocks, r.code), g(3, 3)],
        4: [g(1, 4)],
        5: [g(2, 4)],
        6: [(tabulate, r.sib_blocks, r.sib_code)],
        9: [g(3, 4)],
        10: [(build, 0)],
        12: [(anc_turn,)],
        14: [s(0, 1)],
        18: [(build, 1)],
        19: [s(0, 2)],
        22: [s(1, 1)],
        23: [(totals, 0)],
        26: [(build, 2)],
        27: [s(1, 2)],
        29: [(weigh, 0)],
        30: [s(2, 1)],
        31: [(totals, 1)],
    }.items():
        plan[at // 8][at % 8] = steps
    copies = []
    for h in range(HEADS):
        run(plan[h][0])
        gathers[h].step(5)
        att = Attention(r, kvg[h], h)
        state = att.stage(None, None, None, 0, r.e0)

        def two(i, state):
            for n in range(3):
                pl.when(i == n)(lambda n=n: run(plan[h][1 + 2 * n]))
            state = att.stage(2 * i, r.e0, state, 2 * i + 1, r.e1)
            for n in range(3):
                pl.when(i == n)(lambda n=n: run(plan[h][2 + 2 * n]))
            return att.stage(2 * i + 1, r.e1, state, 2 * i + 2, r.e0)

        if UNROLL:
            for i in range(3):
                run(plan[h][1 + 2 * i])
                state = att.stage(2 * i, r.e0, state, 2 * i + 1, r.e1)
                run(plan[h][2 + 2 * i])
                state = att.stage(2 * i + 1, r.e1, state, 2 * i + 2, r.e0)
        else:
            state = lax.fori_loop(0, 3, two, state)
        run(plan[h][7])
        att.stage(GROUP - 1, r.e0, state, None, None)
        slots_out(h)
        cols = pl.ds(h * GROUP * HEAD, GROUP * HEAD)
        copy = pltpu.make_async_copy(r.dq.at[:, cols], r.dq_hbm.at[:, cols], r.osem.at[h])
        copy.start()
        copies.append(copy)
    run([(build, 3), w(0, 1), s(2, 2), (weigh, 1), s(3, 1)])
    run([(weighed, 0), (totals, 2), w(1, 1), s(3, 2), (weighed, 1), (weigh, 2), (totals, 3)])
    run([w(2, 1), (state_grad,), (weighed, 2), (weigh, 3)])
    copy = pltpu.make_async_copy(r.dstate, r.dstate_hbm, r.osem.at[HEADS])
    copy.start()
    copies.append(copy)
    run([w(3, 1), (weighed, 3)])

    def rows_of(both):
        both = both.reshape(64, HEAD)
        return jnp.where(c == 0, both[0:28], both[28:56])

    for h in range(HEADS):
        finals[h].got(0)
        own, other = rows_of(r.fin[h]), rows_of(r.fin_in[h])
        cols = pl.ds(h * HEAD, HEAD)
        r.gk[:, cols] = jnp.where(c == 0, own, other)
        r.gv[:, cols] = jnp.where(c == 0, other, own)
    for flows in (gathers, scatters, weights, overs, pairs, acrosses, finals, [anc_flow, block_flow]):
        for flow in flows:
            flow.finish()
    for copy in copies:
        copy.wait()


UNROLL = True


def tree_call(blocks, count, anc, wk, wv, q, out, grad, bk, bv):
    hbm = pl.BlockSpec(memory_space=pl.ANY)
    smem = pl.BlockSpec(memory_space=pltpu.SMEM)
    vmem = pl.BlockSpec(memory_space=pltpu.VMEM)
    dma = pltpu.SemaphoreType.DMA

    def bf(*shape):
        return pltpu.VMEM(shape, BF)

    width = HEADS * HEAD
    scratch = [
        bf(OWN, WIDTH), bf(WIDTH, width), bf(WIDTH, width),
        bf(TOK, WIDTH), bf(TOK, WIDTH), bf(TOK, WIDTH),
        bf(2, HEADS, 2, BLK, HEAD),
        *[bf(2, 4, 4, 2, 2, BLK, HEAD)] * HEADS,
        bf(4, 2, OWN, COLS), bf(COLS, 1024),
        bf(KEYS, HEAD), bf(KEYS, HEAD), bf(HEAD, KEYS),
        pltpu.VMEM((HEADS * GROUP, TOK, TOK), F32), pltpu.VMEM((HEADS * GROUP, 1, TOK), F32),
        pltpu.VMEM((HEADS * GROUP, 8, TOK), F32), pltpu.VMEM((HEADS * GROUP, 1, TOK), F32),
        pltpu.VMEM((ANC, TOK), F32), pltpu.VMEM((ANC, TOK), F32),
        pltpu.VMEM((KEYS, HEAD), F32), pltpu.VMEM((KEYS, HEAD), F32),
        bf(TOK, WIDTH),
        *[bf(2, NA, BLK, HEAD)] * HEADS,
        *[bf(NA, BLK, HEAD)] * HEADS,
        bf(HEADS, 4, 4, 2, OWN, HEAD), bf(HEADS, 2, 2, 2, OWN, HEAD), bf(HEADS, 2, 4, 2, OWN, HEAD),
        bf(HEADS, 4, 2, OWN, HEAD), bf(HEADS, 3, 2, OWN, HEAD),
        bf(HEADS, 2, OWN, HEAD), bf(HEADS, OWN, HEAD),
        *[bf(4, 2, OWN, HEAD)] * HEADS,
        bf(HEADS, 4, 4, 2, 32, HEAD), bf(HEADS, 3, 4, 2, 32, HEAD),
        bf(HEADS, 4, 2, 32, HEAD), bf(HEADS, 3, 2, 32, HEAD),
        pltpu.VMEM((HEADS, 2, 32, HEAD), F32), pltpu.VMEM((HEADS, 2, 32, HEAD), F32),
        bf(OWN, WIDTH),
        pltpu.SMEM((32,), jnp.int32), pltpu.SMEM((32,), jnp.int32),
        pltpu.VMEM((1, NA), jnp.int32), pltpu.SMEM((1, NA), jnp.int32),
        dma((1,)), dma((1,)),
        dma((13,)), dma((HEADS + 1,)),
        dma((HEADS, 13)), dma((HEADS, 13)),
        dma((7,)), dma((7,)),
        dma((HEADS, 8)), dma((HEADS, 8)),
        dma((HEADS, 1)), dma((HEADS, 1)),
        dma((HEADS, 1)), dma((HEADS, 1)),
        dma((HEADS, 4)), dma((HEADS, 4)),
        dma((HEADS, 8)), dma((HEADS, 8)),
        dma((HEADS, 1)), dma((HEADS, 1)),
    ]
    return pl.pallas_call(
        tree_kernel,
        out_shape=(
            jax.ShapeDtypeStruct((TOK, WIDTH), BF),
            jax.ShapeDtypeStruct((TOK, width), BF),
            jax.ShapeDtypeStruct((TOK, width), BF),
            jax.ShapeDtypeStruct((OWN, WIDTH), BF),
            jax.ShapeDtypeStruct((28, width), F32),
            jax.ShapeDtypeStruct((28, width), F32),
        ),
        in_specs=[smem, hbm, smem] + [hbm] * 6 + [vmem] * 2,
        out_specs=(hbm, vmem, vmem, hbm, vmem, vmem),
        scratch_shapes=scratch,
        compiler_params=pltpu.CompilerParams(
            collective_id=0, has_side_effects=True, vmem_limit_bytes=60 * MIB
        ),
        name="tree",
    )(blocks, blocks, count, anc, wk, wv, q, out, grad, bk, bv)


def settle_kernel(*refs):
    n = (len(refs) - 2) // 3
    sem_in, sem_out = refs[-2:]
    views = []
    for k in range(n):
        src, dst, held = refs[k], refs[n + k], refs[2 * n + k]
        if k == 0:
            for part in range(4):
                rows = pl.ds(part * (TOK // 4), TOK // 4)
                views.append((src.at[rows], held.at[rows], dst.at[rows]))
        else:
            views.append((src, held, dst))
    ins = [pltpu.make_async_copy(x, y, sem_in.at[k]) for k, (x, y, _) in enumerate(views)]
    outs = [pltpu.make_async_copy(y, z, sem_out.at[k]) for k, (_, y, z) in enumerate(views)]
    for copy in ins:
        copy.start()
    for copy, out in zip(ins, outs, strict=True):
        copy.wait()
        out.start()
    for copy in outs:
        copy.wait()


def settle(arrays):
    hbm = pl.BlockSpec(memory_space=pl.ANY)
    count = len(arrays) + 3
    return pl.pallas_call(
        settle_kernel,
        out_shape=tuple(jax.ShapeDtypeStruct(x.shape, x.dtype) for x in arrays),
        in_specs=[hbm] * len(arrays),
        out_specs=(hbm,) * len(arrays),
        scratch_shapes=[pltpu.VMEM(x.shape, x.dtype) for x in arrays]
        + [pltpu.SemaphoreType.DMA((count,)), pltpu.SemaphoreType.DMA((count,))],
        compiler_params=pltpu.CompilerParams(vmem_limit_bytes=62 * MIB),
        name="settle",
    )(*arrays)


def on_device(q, bk, bv, out, grad, anc, wk, wv, blocks, count):
    return settle(tree_call(blocks, count, anc, wk, wv, q, out, grad, bk, bv))


def solution(mesh):
    rows = P(("dp", "leaf"), None)
    return jax.shard_map(
        on_device,
        mesh=mesh,
        in_specs=(rows, rows, rows, rows, rows, rows, P(), P(), rows, P(("dp", "leaf"))),
        out_specs=(rows,) * 6,
        check_vma=False,
    )
```
